32 devices in a mesh: speech: 4 (over y, core), text: 8 (over z, x).
Axes of the slice: x: 2, y: 2, z: 4, core: 2. Of those that a mesh axis runs over, the one named last changes fastest.
Arguments:
- speech_feat: float32 [2048, 512], P('speech', 'text'), may hold values from -4 to 4
- text_feat: float32 [16384, 512], P(('text', 'speech')), may hold values from -4 to 4
- text_pot: float32 [16384], P('text'), may hold values from -1 to 1
- map_grad: float32 [2048, 512], P('speech', 'text'), may hold values from -1024 to 1024
Outputs:
- speech_grad: float32 [2048, 512], P('speech', 'text')
- text_grad: float32 [16384, 512], P(('text', 'speech'))
The draws below stay inside these ranges and needn't reach their ends.
All inputs are finite; a program needn't handle non-finite values.
Results may differ from the reference program's by a relative error of at most 0.0003.
Values sent between devices are 32-bit elements; how exact they have to be, the bound alone decides.
No kernel may reach another device: no remote copies, remote signals or barrier semaphores. Data moves between devices by JAX's collectives and lax.ppermute only.
A program may use at most 64 MiB of HBM per device.

```python
import math
import jax
import jax.numpy as jnp
from jax import lax

D = 512
SP_DEV = 512
NS = 2048
NT = 16384


def levels(stream_key, shape, split, least, top_value):
    gain = 1.0
    for dim, parts in split:
        heights = jax.random.uniform(jax.random.fold_in(jax.random.fold_in(stream_key, 6), dim), (parts,), jnp.float32, least / len(split), top_value / len(split))
        gain = gain * jnp.repeat(jnp.exp(heights), shape[dim] // parts).reshape((-1,) + (1,) * (len(shape) - 1 - dim))
    return gain


def bell_draw(rng, shape, spread, limit, split=(), kind=jnp.bfloat16):
    values = spread * jax.random.normal(rng, shape, jnp.float32)
    if split:
        values = values * levels(rng, shape, split, -0.22, 0.18)
    return jnp.clip(values, -limit, limit).astype(kind)


def setup_inputs(seed: int = 0) -> dict:
    key_of = jax.random.split(jax.random.key(seed), 5)
    speech_feat = bell_draw(key_of[0], (NS, D), 1.0, 4.0, ((0, 4), (1, 8)), jnp.float32)
    text_feat = bell_draw(key_of[1], (NT, D), 1.0, 4.0, ((0, 32),), jnp.float32)
    text_pot = jnp.clip(jax.random.uniform(key_of[2], (NT,), jnp.float32, -1.0, 1.0) * levels(key_of[2], (NT,), ((0, 8),), -0.4, 0.0), -1.0, 1.0)
    map_grad = bell_draw(key_of[3], (NS, D), (NT / (2 * NS ** 0.5)), 1024.0, ((0, 4), (1, 8)), jnp.float32)
    return dict(speech_feat=speech_feat, text_feat=text_feat, text_pot=text_pot, map_grad=map_grad)


def reference(speech_feat, text_feat, text_pot, map_grad):
    scale = 1.0 / math.sqrt(D)
    highest = lax.Precision.HIGHEST

    def block_step(text_grad, block_index):
        offset = (block_index * SP_DEV).astype(jnp.int32)
        frames = lax.dynamic_slice_in_dim(speech_feat, offset, SP_DEV)
        grads = lax.dynamic_slice_in_dim(map_grad, offset, SP_DEV)
        feat_dots = jnp.dot(frames, text_feat.T, precision=highest, preferred_element_type=jnp.float32)
        grad_dots = jnp.dot(grads, text_feat.T, precision=highest, preferred_element_type=jnp.float32)
        plan_tile = jnp.exp(text_pot[None, :] + scale * feat_dots)
        mass = lax.optimization_barrier(jnp.sum(plan_tile, axis=1))
        first = jnp.dot(plan_tile, text_feat, precision=highest, preferred_element_type=jnp.float32)
        second = jnp.dot(plan_tile * grad_dots, text_feat, precision=highest, preferred_element_type=jnp.float32)
        dots = lax.optimization_barrier(jnp.sum(grads * first, axis=1)) / mass
        speech_block = scale / mass[:, None] * (second - dots[:, None] * first)
        shared = plan_tile / mass[:, None]
        weighted = shared * (grad_dots - dots[:, None])
        added = jnp.dot(shared.T, grads, precision=highest, preferred_element_type=jnp.float32)
        added = added + scale * jnp.dot(weighted.T, frames, precision=highest, preferred_element_type=jnp.float32)
        return (text_grad + added, speech_block)
    text_grad, blocks = lax.scan(block_step, jnp.zeros((NT, D), jnp.float32), jnp.arange(NS // SP_DEV, dtype=jnp.int32))
    return (blocks.reshape(NS, D), text_grad)
```

```python
import functools
import math

import jax
import jax.numpy as jnp
from jax import lax
from jax.experimental import pallas as pl
from jax.experimental.pallas import tpu as pltpu
from jax.sharding import PartitionSpec as P

ROWS = 256
VMEM_LIMIT = 48 * 1024 * 1024


def halves(value):
    high = value.astype(jnp.bfloat16)
    low = (value - high.astype(jnp.float32)).astype(jnp.bfloat16)
    return (high, low)


def dot(left, right, dims):
    return lax.dot_general(left, right, (dims, ((), ())), preferred_element_type=jnp.float32)


def dot3(left, right, dims):
    return dot(left[0], right[0], dims) + dot(left[0], right[1], dims) + dot(left[1], right[0], dims)


def plan_kernel(n_text, n_speech, scale, rows, place, pot, *refs):
    chunks, refs = refs[:n_text], refs[n_text:]
    blocks, refs = refs[:n_speech], refs[n_speech:]
    plan_out, dots_out, sums_out, left_high, left_low, text_high, text_low = refs
    step = pl.program_id(0)
    width = chunks[0].shape[0] // 2
    frames = chunks[0].shape[1]
    block_rows = blocks[0].shape[0]

    @pl.when(step == 0)
    def _():
        me = place[0]
        for k in range(n_text):
            start = pl.multiple_of((me ^ k) * width, width)
            for part in range(2):
                high, low = halves(chunks[k][part * width : (part + 1) * width, :])
                columns = slice(part * frames, (part + 1) * frames)
                left_high[pl.ds(start, width), columns] = high
                left_low[pl.ds(start, width), columns] = low
        for r in range(n_speech):
            high, low = halves(blocks[r][...])
            text_high[r * block_rows : (r + 1) * block_rows, :] = high
            text_low[r * block_rows : (r + 1) * block_rows, :] = low
        sums_out[...] = jnp.zeros_like(sums_out)

    here = pl.ds(pl.multiple_of(step * rows, rows), rows)
    text = (text_high[here, :], text_low[here, :])
    product = dot3(text, (left_high[...], left_low[...]), ((1,), (0,)))
    plan = jnp.exp(pot[...] + scale * product[:, :frames])
    grad_dots = product[:, frames:]
    plan_out[...] = plan
    dots_out[...] = grad_dots
    sums_out[0:1, :] += jnp.sum(plan, axis=0, keepdims=True)
    sums_out[1:2, :] += jnp.sum(plan * grad_dots, axis=0, keepdims=True)


def plan_tiles(place, pot, chunks, blocks, scale):
    n_text, n_speech = len(chunks), len(blocks)
    frames = chunks[0].shape[1]
    feats = blocks[0].shape[1]
    tokens = pot.shape[0]
    rows = math.gcd(ROWS, tokens)
    whole = lambda shape: pl.BlockSpec(shape, lambda i: (0, 0))
    return pl.pallas_call(
        functools.partial(plan_kernel, n_text, n_speech, scale, rows),
        grid=(tokens // rows,),
        in_specs=[
            pl.BlockSpec(memory_space=pltpu.SMEM),
            pl.BlockSpec((rows, 1), lambda i: (i, 0)),
        ]
        + [whole(c.shape) for c in chunks]
        + [whole(b.shape) for b in blocks],
        out_specs=[
            pl.BlockSpec((rows, frames), lambda i: (i, 0)),
            pl.BlockSpec((rows, frames), lambda i: (i, 0)),
            whole((8, frames)),
            whole((feats, 2 * frames)),
            whole((feats, 2 * frames)),
            whole((tokens, feats)),
            whole((tokens, feats)),
        ],
        out_shape=[
            jax.ShapeDtypeStruct((tokens, frames), jnp.float32),
            jax.ShapeDtypeStruct((tokens, frames), jnp.float32),
            jax.ShapeDtypeStruct((8, frames), jnp.float32),
            jax.ShapeDtypeStruct((feats, 2 * frames), jnp.bfloat16),
            jax.ShapeDtypeStruct((feats, 2 * frames), jnp.bfloat16),
            jax.ShapeDtypeStruct((tokens, feats), jnp.bfloat16),
            jax.ShapeDtypeStruct((tokens, feats), jnp.bfloat16),
        ],
        compiler_params=pltpu.CompilerParams(vmem_limit_bytes=VMEM_LIMIT),
        name="plan",
    )(place, pot, *chunks, *blocks)


def weights(sums, plan, grad_dots, scale):
    mass = sums[0:1, :]
    shared = plan / mass
    weighted = scale * (shared * (grad_dots - sums[1:2, :] / mass))
    return (shared, weighted)


def text_kernel(scale, sums, plan, grad_dots, left_high, left_low, out):
    frames = plan.shape[1]
    shared, weighted = weights(sums, plan[...], grad_dots[...], scale)
    shared, weighted = halves(shared), halves(weighted)
    left = (
        jnp.concatenate([weighted[0], shared[0]], axis=1),
        jnp.concatenate([weighted[1], shared[1]], axis=1),
    )
    out[...] = dot3(left, (left_high[...], left_low[...]), ((1,), (1,)))


def text_rows(sums, plan, grad_dots, left, scale, first, count):
    frames = plan.shape[1]
    feats = left[0].shape[0]
    rows = math.gcd(ROWS, count)
    base = first // rows
    whole = lambda shape: pl.BlockSpec(shape, lambda i: (0, 0))
    return pl.pallas_call(
        functools.partial(text_kernel, scale),
        grid=(count // rows,),
        in_specs=[
            whole(sums.shape),
            pl.BlockSpec((rows, frames), lambda i: (base + i, 0)),
            pl.BlockSpec((rows, frames), lambda i: (base + i, 0)),
            whole(left[0].shape),
            whole(left[1].shape),
        ],
        out_specs=pl.BlockSpec((rows, feats), lambda i: (i, 0)),
        out_shape=jax.ShapeDtypeStruct((count, feats), jnp.float32),
        compiler_params=pltpu.CompilerParams(vmem_limit_bytes=VMEM_LIMIT),
        name="text_terms",
    )(sums, plan, grad_dots, *left)


def speech_kernel(n_text, scale, place, sums, plan, grad_dots, text_high, text_low, near, far, total):
    step = pl.program_id(0)
    _, weighted = weights(sums, plan[...], grad_dots[...], scale)
    term = dot3((text_high[...], text_low[...]), halves(weighted), ((0,), (0,)))

    @pl.when(step == 0)
    def _():
        total[...] = term

    @pl.when(step > 0)
    def _():
        total[...] += term

    @pl.when(step == pl.num_programs(0) - 1)
    def _():
        me = place[0]
        width = total.shape[0] // n_text
        for k in range(0, n_text, 2):
            for out, index in ((near, k), (far, k + 1)):
                start = pl.multiple_of((me ^ index) * width, width)
                out[k // 2] = total[pl.ds(start, width), :]


def speech_terms(place, sums, plan, grad_dots, text, scale, n_text):
    tokens, frames = plan.shape
    feats = text[0].shape[1]
    rows = math.gcd(ROWS, tokens)
    shape = (n_text // 2, feats // n_text, frames)
    whole = lambda shape: pl.BlockSpec(shape, lambda i: (0,) * len(shape))
    tile = lambda columns: pl.BlockSpec((rows, columns), lambda i: (i, 0))
    return pl.pallas_call(
        functools.partial(speech_kernel, n_text, scale),
        grid=(tokens // rows,),
        in_specs=[
            pl.BlockSpec(memory_space=pltpu.SMEM),
            whole(sums.shape),
            tile(frames),
            tile(frames),
            tile(feats),
            tile(feats),
        ],
        out_specs=[whole(shape), whole(shape)],
        out_shape=[jax.ShapeDtypeStruct(shape, jnp.float32)] * 2,
        scratch_shapes=[pltpu.VMEM((feats, frames), jnp.float32)],
        compiler_params=pltpu.CompilerParams(vmem_limit_bytes=VMEM_LIMIT),
        name="speech_terms",
    )(place, sums, plan, grad_dots, *text)


def shards(n_speech, n_text, speech_feat, text_feat, text_pot, map_grad):
    def swap(value, axis, k):
        count = {"speech": n_speech, "text": n_text}[axis]
        return lax.ppermute(value, axis, [(i, i ^ k) for i in range(count)])

    feats = text_feat.shape[1]
    scale = 1.0 / math.sqrt(feats)
    rows = text_feat.shape[0]
    t = lax.axis_index("text")
    s = lax.axis_index("speech")
    place = jnp.stack([t, s]).astype(jnp.int32)

    packed = jnp.concatenate([speech_feat.T, map_grad.T], axis=0)
    blocks = [text_feat] + [None] * (n_speech - 1)
    for r in range(2, n_speech, 2):
        blocks[r] = swap(text_feat, "speech", r)
    chunks = [packed] + [None] * (n_text - 1)
    for k in range(2, n_text, 2):
        chunks[k] = swap(packed, "text", k)
    for k in range(0, n_text, 2):
        chunks[k + 1] = swap(chunks[k], "text", 1)
    for r in range(0, n_speech, 2):
        blocks[r + 1] = swap(blocks[r], "speech", 1)
    pot = jnp.concatenate(
        [lax.dynamic_slice_in_dim(text_pot, (s ^ r) * rows, rows) for r in range(n_speech)]
    )[:, None]

    plan, grad_dots, sums, *rest = plan_tiles(place, pot, chunks, blocks, scale)
    left, text = rest[:2], rest[2:]
    step = 1
    while step < n_text:
        sums = sums + swap(sums, "text", step)
        step *= 2

    near, far = speech_terms(place, sums, plan, grad_dots, text, scale, n_text)
    terms = lambda r: text_rows(sums, plan, grad_dots, left, scale, r * rows, rows)
    speech_sum = near + swap(far, "text", 1)
    speech_block = speech_sum[0]
    for k in range(2, n_text, 2):
        speech_block = speech_block + swap(speech_sum[k // 2], "text", k)
    text_grad = None
    for r in [*range(2, n_speech, 2), 0]:
        crossed = swap(terms(r + 1), "speech", 1)
        part = terms(r) + crossed
        part = swap(part, "speech", r) if r else part
        text_grad = part if text_grad is None else text_grad + part
    return (speech_block.T, text_grad)


def solution(mesh):
    body = functools.partial(shards, mesh.shape["speech"], mesh.shape["text"])
    return jax.shard_map(
        body,
        mesh=mesh,
        in_specs=(P("speech", "text"), P(("text", "speech"), None), P("text"), P("speech", "text")),
        out_specs=(P("speech", "text"), P(("text", "speech"), None)),
        check_vma=False,
    )
```

```python
import functools
import math

import jax
import jax.numpy as jnp
from jax import lax
from jax.experimental import pallas as pl
from jax.experimental.pallas import tpu as pltpu
from jax.sharding import PartitionSpec as P

ROWS = 512
VMEM_LIMIT = 16 * 1024 * 1024
LONG = 10**11


def halves(value):
    high = value.astype(jnp.bfloat16)
    low = (value - high.astype(jnp.float32)).astype(jnp.bfloat16)
    return (high, low)


def dot(left, right, dims):
    return lax.dot_general(left, right, (dims, ((), ())), preferred_element_type=jnp.float32)


def dot3(left, right, dims):
    return dot(left[0], right[0], dims) + dot(left[0], right[1], dims) + dot(left[1], right[0], dims)


def whole(shape):
    return pl.BlockSpec(shape, lambda *_: (0,) * len(shape))


def params():
    return pltpu.CompilerParams(vmem_limit_bytes=VMEM_LIMIT)


def cost(macs, moved, exps=0):
    return pl.CostEstimate(flops=6 * macs, bytes_accessed=moved, transcendentals=exps)


def pack_kernel(speech, grad, first, out):
    del first
    width = speech.shape[1]
    out[:width, :] = speech[...].T
    out[width:, :] = grad[...].T


def pack(speech, grad, first):
    frames, width = speech.shape
    in_vmem = pl.BlockSpec(memory_space=pltpu.VMEM)
    return pl.pallas_call(
        pack_kernel,
        in_specs=[in_vmem, in_vmem, pl.BlockSpec(memory_space=pl.ANY)],
        out_shape=jax.ShapeDtypeStruct((2 * width, frames), jnp.float32),
        compiler_params=params(),
        cost_estimate=cost(0, 16 * frames * width),
        name="pack",
    )(speech, grad, first)


def add_kernel(*refs):
    *terms, out = refs
    total = terms[0][...]
    for term in terms[1:]:
        total = total + term[...]
    out[...] = total


def add(*terms):
    return pl.pallas_call(
        add_kernel,
        out_shape=jax.ShapeDtypeStruct(terms[0].shape, terms[0].dtype),
        compiler_params=params(),
        cost_estimate=cost(LONG // 6, 4 * terms[0].size),
        name="add",
    )(*terms)


def split_kernel(block, high_out, low_out, across_high, across_low):
    value = block[...]
    high_out[...], low_out[...] = halves(value)
    across_high[...], across_low[...] = halves(value.T)


def split_block(block):
    rows, feats = block.shape
    return pl.pallas_call(
        split_kernel,
        out_shape=[jax.ShapeDtypeStruct((rows, feats), jnp.bfloat16)] * 2
        + [jax.ShapeDtypeStruct((feats, rows), jnp.bfloat16)] * 2,
        compiler_params=params(),
        cost_estimate=cost(0, 3 * block.size * 4),
        name="split_block",
    )(block)


def assemble(place, chunks, left_high, left_low):
    width = chunks[0].shape[0] // 2
    frames = chunks[0].shape[1]
    for k, chunk in enumerate(chunks):
        start = pl.multiple_of((place[0] ^ k) * width, width)
        for part in range(2):
            high, low = halves(chunk[part * width : (part + 1) * width, :])
            columns = slice(part * frames, (part + 1) * frames)
            left_high[pl.ds(start, width), columns] = high
            left_low[pl.ds(start, width), columns] = low


def plan_rows(scale, pot, blocks, left, plan_out, dots_out, sums_out):
    count = len(blocks) // 2
    frames = plan_out.shape[1]
    block_rows = blocks[0].shape[0]
    rows = math.gcd(ROWS, block_rows)
    for r in range(count):

        @pl.loop(0, block_rows // rows)
        def _(step):
            here = pl.ds(pl.multiple_of(step * rows, rows), rows)
            there = pl.ds(pl.multiple_of(r * block_rows + step * rows, rows), rows)
            text = (blocks[r][here, :], blocks[count + r][here, :])
            product = dot3(text, (left[0][...], left[1][...]), ((1,), (0,)))
            plan = jnp.exp(pot[there, :] + scale * product[:, :frames])
            grad_dots = product[:, frames:]
            plan_out[there, :] = plan
            dots_out[there, :] = grad_dots
            sums_out[0:1, :] += jnp.sum(plan, axis=0, keepdims=True)
            sums_out[1:2, :] += jnp.sum(plan * grad_dots, axis=0, keepdims=True)


def first_kernel(n_text, scale, place, pot, *refs):
    chunks, blocks = refs[:n_text], refs[n_text:-5]
    plan_out, dots_out, sums_out, *left = refs[-5:]
    assemble(place, chunks, *left)
    sums_out[...] = jnp.zeros_like(sums_out)
    plan_rows(scale, pot, blocks, left, plan_out, dots_out, sums_out)


def second_kernel(scale, pot, sums, left_high, left_low, *refs):
    blocks = refs[:-3]
    plan_out, dots_out, sums_out = refs[-3:]
    sums_out[...] = sums[...]
    plan_rows(scale, pot, blocks, (left_high, left_low), plan_out, dots_out, sums_out)


def plan_call(kernel, name, operands, in_smem, tokens, frames, feats, more, flops):
    in_vmem = pl.BlockSpec(memory_space=pltpu.VMEM)
    return pl.pallas_call(
        kernel,
        in_specs=[pl.BlockSpec(memory_space=pltpu.SMEM)] * in_smem + [in_vmem] * (len(operands) - in_smem),
        out_shape=[
            jax.ShapeDtypeStruct((tokens, frames), jnp.float32),
            jax.ShapeDtypeStruct((tokens, frames), jnp.float32),
            jax.ShapeDtypeStruct((8, frames), jnp.float32),
        ]
        + more,
        compiler_params=params(),
        cost_estimate=cost(flops, 16 * tokens * frames, tokens * frames),
        name=name,
    )(*operands)


def plan_tiles(place, pot, chunks, highs, lows, scale):
    n_text, n_speech = len(chunks), len(highs)
    block_rows, feats = highs[0].shape
    frames = chunks[0].shape[1]
    half = n_speech // 2
    tokens = half * block_rows
    left = [jax.ShapeDtypeStruct((feats, 2 * frames), jnp.bfloat16)] * 2
    early = plan_call(
        functools.partial(first_kernel, n_text, scale),
        "plan_early",
        [place, pot[:tokens], *chunks, *highs[:half], *lows[:half]],
        1, tokens, frames, feats, left, LONG // 6,
    )
    late = plan_call(
        functools.partial(second_kernel, scale),
        "plan_late",
        [pot[tokens:], early[2], early[3], early[4], *highs[half:], *lows[half:]],
        0, tokens, frames, feats, [], 2 * tokens * frames * feats,
    )
    return ([early[0], late[0]], [early[1], late[1]], late[2], early[3:])


def across_kernel(high, low, high_out, low_out):
    high_out[...] = high[...].astype(jnp.float32).T.astype(jnp.bfloat16)
    low_out[...] = low[...].astype(jnp.float32).T.astype(jnp.bfloat16)


def frames_first(left):
    rows, columns = left[0].shape
    return pl.pallas_call(
        across_kernel,
        out_shape=[jax.ShapeDtypeStruct((columns, rows), jnp.bfloat16)] * 2,
        compiler_params=params(),
        cost_estimate=cost(0, 8 * rows * columns),
        name="frames_first",
    )(*left)


def weights(sums, plan, grad_dots, scale):
    mass = sums[0:1, :]
    shared = plan / mass
    weighted = scale * (shared * (grad_dots - sums[1:2, :] / mass))
    return (shared, weighted)


def text_kernel(scale, first, sums, plan, grad_dots, right_high, right_low, out):
    here = slice(first, first + out.shape[0])
    shared, weighted = weights(sums, plan[here, :], grad_dots[here, :], scale)
    shared, weighted = halves(shared), halves(weighted)
    left = (
        jnp.concatenate([weighted[0], shared[0]], axis=1),
        jnp.concatenate([weighted[1], shared[1]], axis=1),
    )
    out[...] = dot3(left, (right_high[...], right_low[...]), ((1,), (0,)))


def text_rows(sums, plan, grad_dots, right, scale, first, count):
    frames = plan[0].shape[1]
    feats = right[0].shape[1]
    late, first = divmod(first, plan[0].shape[0])
    return pl.pallas_call(
        functools.partial(text_kernel, scale, first),
        out_shape=jax.ShapeDtypeStruct((count, feats), jnp.float32),
        compiler_params=params(),
        cost_estimate=cost(2 * count * frames * feats, 12 * count * frames),
        name="text_terms",
    )(sums, plan[late], grad_dots[late], *right)


def speech_kernel(n_text, scale, place, sums, *refs):
    plans, refs = refs[:2], refs[2:]
    dots, refs = refs[:2], refs[2:]
    *blocks, near, far, total = refs
    count = len(blocks) // 2
    rows = blocks[0].shape[1]
    for r in range(count):
        late, start = divmod(r * rows, plans[0].shape[0])
        here = slice(start, start + rows)
        _, weighted = weights(sums, plans[late][here, :], dots[late][here, :], scale)
        term = dot3((blocks[r][...], blocks[count + r][...]), halves(weighted), ((1,), (0,)))
        if r:
            total[...] += term
        else:
            total[...] = term
    width = total.shape[0] // n_text
    for k in range(0, n_text, 2):
        for out, index in ((near, k), (far, k + 1)):
            start = pl.multiple_of((place[0] ^ index) * width, width)
            out[k // 2] = total[pl.ds(start, width), :]


def speech_terms(place, sums, plans, dots, highs, lows, scale, n_text):
    frames = plans[0].shape[1]
    n_speech, (feats, rows) = len(highs), highs[0].shape
    shape = (n_text // 2, feats // n_text, frames)
    in_vmem = pl.BlockSpec(memory_space=pltpu.VMEM)
    return pl.pallas_call(
        functools.partial(speech_kernel, n_text, scale),
        in_specs=[pl.BlockSpec(memory_space=pltpu.SMEM)] + [in_vmem] * (5 + 2 * n_speech),
        out_shape=[jax.ShapeDtypeStruct(shape, jnp.float32)] * 2,
        scratch_shapes=[pltpu.VMEM((feats, frames), jnp.float32)],
        compiler_params=params(),
        cost_estimate=cost(n_speech * rows * frames * feats, 12 * n_speech * rows * frames),
        name="speech_terms",
    )(place, sums, *plans, *dots, *highs, *lows)


def shards(n_speech, n_text, speech_feat, text_feat, text_pot, map_grad):
    def swap(value, axis, k):
        count = {"speech": n_speech, "text": n_text}[axis]
        return lax.ppermute(value, axis, [(i, i ^ k) for i in range(count)])

    feats = text_feat.shape[1]
    scale = 1.0 / math.sqrt(feats)
    rows = text_feat.shape[0]
    t = lax.axis_index("text")
    s = lax.axis_index("speech")
    place = jnp.stack([t, s]).astype(jnp.int32)

    blocks = [text_feat] + [None] * (n_speech - 1)
    for r in range(2, n_speech, 2):
        blocks[r] = swap(text_feat, "speech", r)
    blocks[1] = swap(text_feat, "speech", 1)
    packed = pack(speech_feat, map_grad, blocks[1])
    chunks = [packed] + [None] * (n_text - 1)
    for k in range(2, n_text, 2):
        chunks[k] = swap(packed, "text", k)
    for k in range(0, n_text, 2):
        chunks[k + 1] = swap(chunks[k], "text", 1)
    for r in range(2, n_speech, 2):
        blocks[r + 1] = swap(blocks[r], "speech", 1)
    highs, lows, across_highs, across_lows = zip(*map(split_block, blocks))
    pot = jnp.concatenate(
        [lax.dynamic_slice_in_dim(text_pot, (s ^ r) * rows, rows) for r in range(n_speech)]
    )[:, None]

    plan, grad_dots, sums, left = plan_tiles(place, pot, chunks, highs, lows, scale)
    right = frames_first(left)
    step = 1
    while step < n_text:
        sums = sums + swap(sums, "text", step)
        step *= 2

    def text_part(r):
        return text_rows(sums, plan, grad_dots, right, scale, r * rows, rows)

    others = []
    for r in range(2, n_speech, 2):
        crossed = swap(text_part(r + 1), "speech", 1)
        others.append(swap(text_part(r) + crossed, "speech", r))
    near, far = speech_terms(place, sums, plan, grad_dots, across_highs, across_lows, scale, n_text)
    speech_sum = near + swap(far, "text", 1)
    speech_block = speech_sum[0]
    for k in range(2, n_text, 2):
        speech_block = speech_block + swap(speech_sum[k // 2], "text", k)
    crossed = swap(text_part(1), "speech", 1)
    text_grad = add(text_part(0), crossed, *others)
    return (speech_block.T, text_grad)


def solution(mesh):
    body = functools.partial(shards, mesh.shape["speech"], mesh.shape["text"])
    return jax.shard_map(
        body,
        mesh=mesh,
        in_specs=(P("speech", "text"), P(("text", "speech"), None), P("text"), P("speech", "text")),
        out_specs=(P("speech", "text"), P(("text", "speech"), None)),
        check_vma=False,
    )
```

```python
import functools
import math

import jax
import jax.numpy as jnp
from jax import lax
from jax.experimental import pallas as pl
from jax.experimental.pallas import tpu as pltpu
from jax.sharding import PartitionSpec as P

LONG, SHORT = 10**11, 10**9
WORK = {
    "plan_early": LONG,
    "plan_late": 3 * SHORT,
    "moments": 3 * SHORT,
    "text_far": 3 * SHORT,
    "text_near": 3 * SHORT,
    "finish": SHORT,
    "frames_first": SHORT,
    "split": SHORT // 2,
    "offsets": SHORT // 10,
    "add": LONG,
}
VMEM_LIMIT = 16 * 1024 * 1024
LANES = 128
IN_VMEM = pl.BlockSpec(memory_space=pltpu.VMEM)
IN_SMEM = pl.BlockSpec(memory_space=pltpu.SMEM)
ANYWHERE = pl.BlockSpec(memory_space=pl.ANY)


def halves(value):
    high = value.astype(jnp.bfloat16)
    low = (value - high.astype(jnp.float32)).astype(jnp.bfloat16)
    return (high, low)


def dot(left, right):
    return lax.dot_general(left, right, (((1,), (0,)), ((), ())), preferred_element_type=jnp.float32)


def dot3(left, right):
    return dot(left[0], right[0]) + dot(left[0], right[1]) + dot(left[1], right[0])


def call(kernel, name, operands, outs, places=0, before=(), scratch=()):
    several = isinstance(outs, list)
    shapes = [jax.ShapeDtypeStruct(shape, kind) for shape, kind in (outs if several else [outs])]
    count = len(operands)

    def body(*refs):
        kernel(*refs[:count], *refs[count + len(before) :])

    return pl.pallas_call(
        body,
        in_specs=[IN_SMEM] * places + [IN_VMEM] * (count - places) + [ANYWHERE] * len(before),
        out_shape=shapes if several else shapes[0],
        scratch_shapes=list(scratch),
        compiler_params=pltpu.CompilerParams(vmem_limit_bytes=VMEM_LIMIT),
        cost_estimate=pl.CostEstimate(flops=WORK.get(name, 0), bytes_accessed=0, transcendentals=0),
        name=name,
    )(*operands, *before)


def copy_kernel(value, out):
    out[...] = value[...]


def add_kernel(*refs):
    *terms, out = refs
    total = terms[0][...]
    for term in terms[1:]:
        total = total + term[...]
    out[...] = total


def split_kernel(block, high_out, low_out, across_high, across_low):
    value = block[...]
    high_out[...], low_out[...] = halves(value)
    across_high[...], across_low[...] = halves(value.T)


def split_block(block):
    rows, feats = block.shape
    plain, across = ((rows, feats), jnp.bfloat16), ((feats, rows), jnp.bfloat16)
    return call(split_kernel, "split", [block], [plain, plain, across, across])


def assemble(place, speech_chunks, grad_chunks, left):
    frames = speech_chunks[0].shape[1]
    for part, chunks in enumerate((speech_chunks, grad_chunks)):
        columns = slice(part * frames, (part + 1) * frames)
        for k, chunk in enumerate(chunks):
            width = chunk.shape[0]
            start = pl.multiple_of((place[0] ^ k) * width, width)
            left[0][pl.ds(start, width), columns], left[1][pl.ds(start, width), columns] = halves(chunk[...])


def offsets_kernel(place, pot, out):
    count, rows = pot.shape
    for r in range(count):
        row = pot[pl.ds(place[1] ^ r, 1), :]
        out[r * rows : (r + 1) * rows, :] = jnp.broadcast_to(row, (out.shape[1], rows)).T


def plan_rows(scale, place, first, pot, blocks, left, plan_out, dots_out, sums_out):
    count = len(blocks) // 2
    frames = plan_out.shape[1]
    rows = blocks[0].shape[0]
    for r in range(count):
        here = slice(r * rows, (r + 1) * rows)
        product = dot3((blocks[r][...], blocks[count + r][...]), (left[0][...], left[1][...]))
        offsets = pot[(first + r) * rows : (first + r + 1) * rows, :]
        lanes = offsets.shape[1]
        plan = jnp.concatenate(
            [jnp.exp(offsets + scale * product[:, i : i + lanes]) for i in range(0, frames, lanes)], axis=1
        )
        grad_dots = product[:, frames:]
        plan_out[here, :] = plan
        dots_out[here, :] = grad_dots
        sums_out[0:1, :] += jnp.sum(plan, axis=0, keepdims=True)
        sums_out[1:2, :] += jnp.sum(plan * grad_dots, axis=0, keepdims=True)


def early_kernel(n_text, scale, place, pot, *refs):
    chunks, blocks = refs[:n_text], refs[n_text:-5]
    plan_out, dots_out, sums_out, *left = refs[-5:]
    width = chunks[0].shape[0] // 2
    assemble(place, [chunk.at[:width] for chunk in chunks], [chunk.at[width:] for chunk in chunks], left)
    sums_out[...] = jnp.zeros_like(sums_out)
    plan_rows(scale, place, 0, pot, blocks, left, plan_out, dots_out, sums_out)


def late_kernel(scale, first, place, pot, sums, left_high, left_low, *refs):
    blocks = refs[:-3]
    plan_out, dots_out, sums_out = refs[-3:]
    sums_out[...] = sums[...]
    plan_rows(scale, place, first, pot, blocks, (left_high, left_low), plan_out, dots_out, sums_out)


def across_kernel(high, low, high_out, low_out):
    for value, out in ((high, high_out), (low, low_out)):
        out[...] = value[...].astype(jnp.float32).T.astype(jnp.bfloat16)


def weights(sums, plan, grad_dots, scale):
    mass = sums[0:1, :]
    shared = plan / mass
    weighted = scale * (shared * (grad_dots - sums[1:2, :] / mass))
    return (shared, weighted)


def text_kernel(scale, first, sums, plan, grad_dots, right_high, right_low, *outs):
    rows = len(outs) * outs[0].shape[0]
    here = slice(first, first + rows)
    shared, weighted = weights(sums, plan[here, :], grad_dots[here, :], scale)
    shared, weighted = halves(shared), halves(weighted)
    left = [jnp.concatenate([w, s], axis=1) for w, s in zip(weighted, shared)]
    terms = dot3(left, (right_high[...], right_low[...]))
    for i, out in enumerate(outs):
        out[...] = terms[i * out.shape[0] : (i + 1) * out.shape[0], :]


def moments_kernel(first, rows, estimate, plan, grad_dots, high, low, *refs):
    *total, out = refs
    here = slice(first, first + rows)
    tile = plan[here, :]
    centred = tile * (grad_dots[here, :] - estimate[1:2, :] / estimate[0:1, :])
    term = dot3((high[...], low[...]), halves(jnp.concatenate([tile, centred], axis=1)))
    out[...] = total[0][...] + term if total else term


def finish_kernel(n_text, scale, first, place, estimate, sums, total, plan, grad_dots, high, low, near, far, terms):
    frames = sums.shape[1]
    mass = sums[0:1, :]
    drift = sums[1:2, :] / mass - estimate[1:2, :] / estimate[0:1, :]
    here = slice(first, first + high.shape[1])
    _, weighted = weights(sums, plan[here, :], grad_dots[here, :], scale)
    terms[...] = dot3((high[...], low[...]), halves(weighted))
    width = total.shape[0] // n_text
    for k in range(n_text):
        here = pl.ds(pl.multiple_of((place[0] ^ k) * width, width), width)
        block = (scale / mass) * (total[here, frames:] - drift * total[here, :frames])
        (far if k % 2 else near)[k // 2] = block + terms[here, :]


def shards(n_speech, n_text, speech_feat, text_feat, text_pot, map_grad):
    def swap(value, axis, k):
        count = {"speech": n_speech, "text": n_text}[axis]
        return lax.ppermute(value, axis, [(i, i ^ k) for i in range(count)])

    rows, feats = text_feat.shape
    frames, width = speech_feat.shape
    scale = 1.0 / math.sqrt(feats)
    place = jnp.stack([lax.axis_index("text"), lax.axis_index("speech")]).astype(jnp.int32)
    pot = call(
        offsets_kernel,
        "offsets",
        [place, text_pot.reshape(n_speech, rows)],
        ((n_speech * rows, LANES), jnp.float32),
        places=1,
    )

    blocks = [text_feat] + [None] * (n_speech - 1)
    for r in range(2, n_speech, 2):
        blocks[r] = swap(text_feat, "speech", r)
    blocks[1] = swap(text_feat, "speech", 1)
    packed = jnp.concatenate([speech_feat.T, map_grad.T], axis=0)
    packed = call(copy_kernel, "copy", [packed], (packed.shape, packed.dtype), before=[blocks[1]])
    chunks = [packed] + [None] * (n_text - 1)
    for k in range(1, n_text):
        if k & (k - 1) == 0:
            chunks[k] = swap(packed, "text", k)
    for k in range(3, n_text):
        if k & (k - 1):
            step = k & -k
            source = chunks[k ^ step]
            wanted = [chunks[1], chunks[2]] if step > 1 else [chunks[3]] if 3 < k == n_text - 1 else []
            if wanted:
                source = call(copy_kernel, "copy", [source], (source.shape, source.dtype), before=wanted)
            chunks[k] = swap(source, "text", step)
    for r in range(2, n_speech, 2):
        blocks[r + 1] = swap(blocks[r], "speech", 1)
    highs, lows, across_highs, across_lows = zip(*map(split_block, blocks))

    half = n_speech // 2
    tile = ((half * rows, frames), jnp.float32)
    outs = [tile, tile, ((8, frames), jnp.float32)]
    left_shape = ((feats, 2 * frames), jnp.bfloat16)
    plan_early, dots_early, sums, *left = call(
        functools.partial(early_kernel, n_text, scale),
        "plan_early",
        [place, pot, *chunks, *highs[:half], *lows[:half]],
        [*outs, left_shape, left_shape],
        places=1,
    )
    plan_late, dots_late, sums = call(
        functools.partial(late_kernel, scale, half),
        "plan_late",
        [place, pot, sums, *left, *highs[half:], *lows[half:]],
        outs,
        places=1,
    )
    plans, dots = (plan_early, plan_late), (dots_early, dots_late)
    right = call(across_kernel, "frames_first", [*left], [(left_shape[0][::-1], jnp.bfloat16)] * 2, before=[sums])

    estimate = sums
    total = []
    step = 1
    for r in range(n_speech):
        if r < n_speech - 1:
            total = [
                call(
                    functools.partial(moments_kernel, r % half * rows, rows),
                    "moments",
                    [estimate, plans[r // half], dots[r // half], across_highs[r], across_lows[r], *total],
                    ((feats, 2 * frames), jnp.float32),
                    before=[sums],
                )
            ]
        if step < n_text:
            crossing = swap(sums, "text", step)
            sums = call(add_kernel, "hop", [sums, crossing], ((8, frames), jnp.float32), before=total)
            step *= 2
    while step < n_text:
        sums = sums + swap(sums, "text", step)
        step *= 2

    def text_part(r, name, before, pieces=1):
        late, first = divmod(r * rows, half * rows)
        return call(
            functools.partial(text_kernel, scale, first),
            name,
            [sums, plans[late], dots[late], *right],
            [((rows // pieces, feats), jnp.float32)] * pieces,
            before=before,
        )

    shape = ((n_text // 2, width, frames), jnp.float32)

    others = []
    for r in range(2, n_speech, 2):
        (term,) = text_part(r + 1, "text_far", [])
        (part,) = text_part(r, "text_far", [term])
        part = part + swap(term, "speech", 1)
        others.append(swap(part, "speech", r))
    near, far = call(
        functools.partial(finish_kernel, n_text, scale, (half - 1) * rows),
        "finish",
        [place, estimate, sums, *total, plans[1], dots[1], across_highs[-1], across_lows[-1]],
        [shape, shape],
        places=1,
        before=[term],
        scratch=[pltpu.VMEM((feats, frames), jnp.float32)],
    )
    crossed = [swap(piece, "speech", 1) for piece in text_part(1, "text_near", [part], 2)]
    near = call(
        pieces_kernel,
        "near",
        [near, swap(far, "text", 1)],
        [((width, frames), jnp.float32)] * (n_text // 2),
        before=crossed,
    )
    speech_terms = [near[0]] + [swap(near[k // 2], "text", k) for k in range(2, n_text, 2)]
    (own,) = text_part(0, "text_near", [part])
    text_grad = call(sum_kernel, "add", [own, *others, *crossed], ((rows, feats), jnp.float32))
    speech_block = call(add_kernel, "join", speech_terms, ((width, frames), jnp.float32), before=[own])
    return (speech_block.T, text_grad)


def pieces_kernel(left, right, *outs):
    for i, out in enumerate(outs):
        out[...] = left[i] + right[i]


def sum_kernel(*refs):
    *terms, out = refs
    rows = out.shape[0]
    total = terms[0][...]
    pieces = [term for term in terms if term.shape[0] < rows]
    for term in terms[1 : len(terms) - len(pieces)]:
        total = total + term[...]
    count = rows // len(pieces)
    for i, piece in enumerate(pieces):
        here = slice(i * count, (i + 1) * count)
        out[here, :] = total[here, :] + piece[...]


def solution(mesh):
    body = functools.partial(shards, mesh.shape["speech"], mesh.shape["text"])
    return jax.shard_map(
        body,
        mesh=mesh,
        in_specs=(P("speech", "text"), P(("text", "speech"), None), P("text"), P("speech", "text")),
        out_specs=(P("speech", "text"), P(("text", "speech"), None)),
        check_vma=False,
    )
```

```python
import functools
import math

import jax
import jax.numpy as jnp
from jax import lax
from jax.experimental import pallas as pl
from jax.experimental.pallas import tpu as pltpu
from jax.sharding import PartitionSpec as P

LONG, SHORT = 10**11, 10**9
WORK = {
    "plan_early": LONG,
    "plan_late": 3 * SHORT,
    "plan_part": SHORT,
    "plan_more": SHORT,
    "moments": 3 * SHORT,
    "text_far": 3 * SHORT,
    "text_near": 3 * SHORT,
    "finish": SHORT,
    "frames_first": SHORT,
    "split": SHORT,
    "offsets": SHORT // 10,
    "add": LONG,
}
VMEM_LIMIT = 16 * 1024 * 1024
LANES = 128
IN_VMEM = pl.BlockSpec(memory_space=pltpu.VMEM)
IN_SMEM = pl.BlockSpec(memory_space=pltpu.SMEM)
ANYWHERE = pl.BlockSpec(memory_space=pl.ANY)


def halves(value):
    high = value.astype(jnp.bfloat16)
    low = (value - high.astype(jnp.float32)).astype(jnp.bfloat16)
    return (high, low)


def dot(left, right):
    return lax.dot_general(left, right, (((1,), (0,)), ((), ())), preferred_element_type=jnp.float32)


def dot3(left, right):
    return dot(left[0], right[0]) + dot(left[0], right[1]) + dot(left[1], right[0])


def call(kernel, name, operands, outs, places=0, before=(), scratch=()):
    several = isinstance(outs, list)
    shapes = [jax.ShapeDtypeStruct(shape, kind) for shape, kind in (outs if several else [outs])]
    count = len(operands)

    def body(*refs):
        kernel(*refs[:count], *refs[count + len(before) :])

    return pl.pallas_call(
        body,
        in_specs=[IN_SMEM] * places + [IN_VMEM] * (count - places) + [ANYWHERE] * len(before),
        out_shape=shapes if several else shapes[0],
        scratch_shapes=list(scratch),
        compiler_params=pltpu.CompilerParams(vmem_limit_bytes=VMEM_LIMIT),
        cost_estimate=pl.CostEstimate(flops=WORK.get(name, 0), bytes_accessed=0, transcendentals=0),
        name=name,
    )(*operands, *before)


def copy_kernel(value, out):
    out[...] = value[...]


def add_kernel(*refs):
    *terms, out = refs
    total = terms[0][...]
    for term in terms[1:]:
        total = total + term[...]
    out[...] = total


def group_of(n_text, width):
    return min(n_text, max(2, LANES // width))


def group_starts(place, group, width, n_text):
    mine = place[0] - place[0] % group
    return [pl.multiple_of((mine ^ first) * width, group * width) for first in range(0, n_text, group)]


def split_kernel(n_text, group, place, block, high_out, low_out, across_high, across_low):
    value = block[...]
    across_high[...], across_low[...] = halves(value.T)
    lanes = block.shape[1] // n_text * group
    for i, start in enumerate(group_starts(place, group, lanes // group, n_text)):
        columns = slice(i * lanes, (i + 1) * lanes)
        high_out[:, columns], low_out[:, columns] = halves(block[:, pl.ds(start, lanes)])


def split_block(place, block, n_text):
    rows, feats = block.shape
    group = group_of(n_text, feats // n_text)
    plain, across = ((rows, feats), jnp.bfloat16), ((feats, rows), jnp.bfloat16)
    body = functools.partial(split_kernel, n_text, group)
    return call(body, "split", [place, block], [plain, plain, across, across], places=1)


def assemble(place, group, first, chunks, left):
    width, frames = chunks[0].shape[0] // 2, chunks[0].shape[1]
    for k, chunk in enumerate(chunks, first):
        row = (k - k % group) * width + (place[0] ^ k) % group * width
        here = pl.ds(pl.multiple_of(row, width), width)
        for part in range(2):
            columns = slice(part * frames, (part + 1) * frames)
            left[0][here, columns], left[1][here, columns] = halves(chunk[part * width : (part + 1) * width, :])


def offsets_kernel(place, pot, out):
    count, rows = pot.shape
    for r in range(count):
        row = pot[pl.ds(place[1] ^ r, 1), :]
        out[r * rows : (r + 1) * rows, :] = jnp.broadcast_to(row, (out.shape[1], rows)).T


def plan_rows(scale, first, pot, blocks, left, partials, plan_out, dots_out, sums_out):
    count = len(blocks) // 2
    frames = plan_out.shape[1]
    rows = blocks[0].shape[0]
    for r in range(count):
        here = slice(r * rows, (r + 1) * rows)
        known = left[0].shape[0] // 2 if r < len(partials) else 0
        text = (blocks[r][:, known:], blocks[count + r][:, known:])
        product = dot3(text, (left[0][known:, :], left[1][known:, :]))
        if known:
            product = product + partials[r][...]
        offsets = pot[(first + r) * rows : (first + r + 1) * rows, :]
        lanes = offsets.shape[1]
        plan = jnp.concatenate(
            [jnp.exp(offsets + scale * product[:, i : i + lanes]) for i in range(0, frames, lanes)], axis=1
        )
        grad_dots = product[:, frames:]
        plan_out[here, :] = plan
        dots_out[here, :] = grad_dots
        sums_out[0:1, :] += jnp.sum(plan, axis=0, keepdims=True)
        sums_out[1:2, :] += jnp.sum(plan * grad_dots, axis=0, keepdims=True)


def part_kernel(n_chunks, group, place, *refs):
    chunks, refs = refs[:n_chunks], refs[n_chunks:]
    count = (len(refs) - 2) // 3
    blocks, outs, left = refs[: 2 * count], refs[2 * count : -2], refs[-2:]
    assemble(place, group, 0, chunks, left)
    known = left[0].shape[0]
    for r in range(count):
        text = (blocks[r][:, :known], blocks[count + r][:, :known])
        outs[r][...] = dot3(text, (left[0][...], left[1][...]))


def more_kernel(left_high, left_low, high, low, out):
    known = left_high.shape[0]
    out[...] = dot3((high[:, :known], low[:, :known]), (left_high[...], left_low[...]))


def early_kernel(n_chunks, n_partials, group, scale, place, pot, *refs):
    known, refs = refs[:2], refs[2:]
    chunks, refs = refs[:n_chunks], refs[n_chunks:]
    partials, blocks = refs[:n_partials], refs[n_partials:-5]
    plan_out, dots_out, sums_out, *left = refs[-5:]
    for old, new in zip(known, left):
        new[: old.shape[0], :] = old[...]
    assemble(place, group, n_chunks, chunks, left)
    sums_out[...] = jnp.zeros_like(sums_out)
    plan_rows(scale, 0, pot, blocks, left, partials, plan_out, dots_out, sums_out)


def late_kernel(n_partials, scale, first, pot, sums, left_high, left_low, *refs):
    partials, blocks = refs[:n_partials], refs[n_partials:-3]
    plan_out, dots_out, sums_out = refs[-3:]
    sums_out[...] = sums[...]
    plan_rows(scale, first, pot, blocks, (left_high, left_low), partials, plan_out, dots_out, sums_out)


def across_kernel(n_text, group, place, high, low, high_out, low_out):
    lanes = high.shape[0] // n_text * group
    starts = group_starts(place, group, lanes // group, n_text)
    for value, out in ((high, high_out), (low, low_out)):
        ordered = jnp.concatenate([value[pl.ds(start, lanes), :] for start in starts], axis=0)
        out[...] = ordered.astype(jnp.float32).T.astype(jnp.bfloat16)


def weights(sums, plan, grad_dots, scale):
    mass = sums[0:1, :]
    shared = plan / mass
    weighted = scale * (shared * (grad_dots - sums[1:2, :] / mass))
    return (shared, weighted)


def text_kernel(scale, first, sums, plan, grad_dots, right_high, right_low, *outs):
    rows = len(outs) * outs[0].shape[0]
    here = slice(first, first + rows)
    shared, weighted = weights(sums, plan[here, :], grad_dots[here, :], scale)
    shared, weighted = halves(shared), halves(weighted)
    left = [jnp.concatenate([w, s], axis=1) for w, s in zip(weighted, shared)]
    terms = dot3(left, (right_high[...], right_low[...]))
    for i, out in enumerate(outs):
        out[...] = terms[i * out.shape[0] : (i + 1) * out.shape[0], :]


def moments_kernel(first, rows, estimate, plan, grad_dots, high, low, *refs):
    *total, out = refs
    here = slice(first, first + rows)
    tile = plan[here, :]
    centred = tile * (grad_dots[here, :] - estimate[1:2, :] / estimate[0:1, :])
    term = dot3((high[...], low[...]), halves(jnp.concatenate([tile, centred], axis=1)))
    out[...] = total[0][...] + term if total else term


def finish_kernel(n_text, scale, first, place, estimate, sums, total, plan, grad_dots, high, low, near, far, terms):
    frames = sums.shape[1]
    mass = sums[0:1, :]
    drift = sums[1:2, :] / mass - estimate[1:2, :] / estimate[0:1, :]
    here = slice(first, first + high.shape[1])
    _, weighted = weights(sums, plan[here, :], grad_dots[here, :], scale)
    terms[...] = dot3((high[...], low[...]), halves(weighted))
    width = total.shape[0] // n_text
    for k in range(n_text):
        here = pl.ds(pl.multiple_of((place[0] ^ k) * width, width), width)
        block = (scale / mass) * (total[here, frames:] - drift * total[here, :frames])
        (far if k % 2 else near)[k // 2] = block + terms[here, :]


def shards(n_speech, n_text, speech_feat, text_feat, text_pot, map_grad):
    def swap(value, axis, k):
        count = {"speech": n_speech, "text": n_text}[axis]
        return lax.ppermute(value, axis, [(i, i ^ k) for i in range(count)])

    rows, feats = text_feat.shape
    frames, width = speech_feat.shape
    scale = 1.0 / math.sqrt(feats)
    place = jnp.stack([lax.axis_index("text"), lax.axis_index("speech")]).astype(jnp.int32)
    pot = call(
        offsets_kernel,
        "offsets",
        [place, text_pot.reshape(n_speech, rows)],
        ((n_speech * rows, LANES), jnp.float32),
        places=1,
    )

    blocks = [text_feat] + [None] * (n_speech - 1)
    for r in range(2, n_speech, 2):
        blocks[r] = swap(text_feat, "speech", r)
    blocks[1] = swap(text_feat, "speech", 1)
    packed = jnp.concatenate([speech_feat.T, map_grad.T], axis=0)
    packed = call(copy_kernel, "copy", [packed], (packed.shape, packed.dtype), before=[blocks[1]])
    chunks = [packed] + [None] * (n_text - 1)
    split = [split_block(place, blocks[0], n_text), split_block(place, blocks[1], n_text)]
    known, group = n_text // 2, group_of(n_text, width)
    part_tile = ((rows, 2 * frames), jnp.float32)
    part_shape = ((feats // 2, 2 * frames), jnp.bfloat16)
    for k in range(1, n_text):
        if k & (k - 1) == 0:
            chunks[k] = swap(packed, "text", k)
    for k in range(3, n_text):
        if k & (k - 1):
            step = k & -k
            source = chunks[k ^ step]
            wanted = [chunks[1], chunks[2], pot, *(block[0] for block in split)] if step > 1 else []
            if k == n_text - 1:
                *partials, part_high, part_low = call(
                    functools.partial(part_kernel, known, group),
                    "plan_part",
                    [place, *chunks[:known], *(block[0] for block in split), *(block[1] for block in split)],
                    [part_tile] * len(split) + [part_shape, part_shape],
                    places=1,
                )
                wanted = [*wanted, part_high]
            if wanted:
                source = call(copy_kernel, "copy", [source], (source.shape, source.dtype), before=wanted)
            chunks[k] = swap(source, "text", step)
    for r in range(2, n_speech, 2):
        blocks[r + 1] = swap(blocks[r], "speech", 1)
    split += [split_block(place, block, n_text) for block in blocks[2:]]
    highs, lows, across_highs, across_lows = zip(*split)
    for r in range(2, min(n_speech, 3)):
        partials.append(call(more_kernel, "plan_more", [part_high, part_low, highs[r], lows[r]], part_tile))

    half = n_speech // 2
    tile = ((half * rows, frames), jnp.float32)
    outs = [tile, tile, ((8, frames), jnp.float32)]
    left_shape = ((feats, 2 * frames), jnp.bfloat16)
    plan_early, dots_early, sums, *left = call(
        functools.partial(early_kernel, n_text - known, len(partials[:half]), group, scale),
        "plan_early",
        [place, pot, part_high, part_low, *chunks[known:], *partials[:half], *highs[:half], *lows[:half]],
        [*outs, left_shape, left_shape],
        places=1,
    )
    plan_late, dots_late, sums = call(
        functools.partial(late_kernel, len(partials[half:]), scale, half),
        "plan_late",
        [pot, sums, *left, *partials[half:], *highs[half:], *lows[half:]],
        outs,
    )
    plans, dots = (plan_early, plan_late), (dots_early, dots_late)
    right = call(
        functools.partial(across_kernel, n_text, group),
        "frames_first",
        [place, *left],
        [(left_shape[0][::-1], jnp.bfloat16)] * 2,
        places=1,
        before=[sums],
    )

    estimate = sums
    total = []
    step = 1
    for r in range(n_speech):
        if r < n_speech - 1:
            total = [
                call(
                    functools.partial(moments_kernel, r % half * rows, rows),
                    "moments",
                    [estimate, plans[r // half], dots[r // half], across_highs[r], across_lows[r], *total],
                    ((feats, 2 * frames), jnp.float32),
                    before=[sums],
                )
            ]
        if step < n_text:
            crossing = swap(sums, "text", step)
            sums = call(add_kernel, "hop", [sums, crossing], ((8, frames), jnp.float32), before=total)
            step *= 2
    while step < n_text:
        sums = sums + swap(sums, "text", step)
        step *= 2

    def text_part(r, name, before, pieces=1):
        late, first = divmod(r * rows, half * rows)
        return call(
            functools.partial(text_kernel, scale, first),
            name,
            [sums, plans[late], dots[late], *right],
            [((rows // pieces, feats), jnp.float32)] * pieces,
            before=before,
        )

    shape = ((n_text // 2, width, frames), jnp.float32)

    others = []
    for r in range(2, n_speech, 2):
        (term,) = text_part(r + 1, "text_far", [])
        (part,) = text_part(r, "text_far", [term])
        part = part + swap(term, "speech", 1)
        others.append(swap(part, "speech", r))
    near, far = call(
        functools.partial(finish_kernel, n_text, scale, (half - 1) * rows),
        "finish",
        [place, estimate, sums, *total, plans[1], dots[1], across_highs[-1], across_lows[-1]],
        [shape, shape],
        places=1,
        before=[term],
        scratch=[pltpu.VMEM((feats, frames), jnp.float32)],
    )
    crossed = [swap(piece, "speech", 1) for piece in text_part(1, "text_near", [part], 2)]
    near = call(
        pieces_kernel,
        "near",
        [near, swap(far, "text", 1)],
        [((width, frames), jnp.float32)] * (n_text // 2),
        before=crossed,
    )
    speech_terms = [near[0]] + [swap(near[k // 2], "text", k) for k in range(2, n_text, 2)]
    (own,) = text_part(0, "text_near", [part])
    text_grad = call(sum_kernel, "add", [own, *others, *crossed], ((rows, feats), jnp.float32))
    speech_block = call(add_kernel, "join", speech_terms, ((width, frames), jnp.float32), before=[own])
    return (speech_block.T, text_grad)


def pieces_kernel(left, right, *outs):
    for i, out in enumerate(outs):
        out[...] = left[i] + right[i]


def sum_kernel(*refs):
    *terms, out = refs
    rows = out.shape[0]
    total = terms[0][...]
    pieces = [term for term in terms if term.shape[0] < rows]
    for term in terms[1 : len(terms) - len(pieces)]:
        total = total + term[...]
    count = rows // len(pieces)
    for i, piece in enumerate(pieces):
        here = slice(i * count, (i + 1) * count)
        out[here, :] = total[here, :] + piece[...]


def solution(mesh):
    body = functools.partial(shards, mesh.shape["speech"], mesh.shape["text"])
    return jax.shard_map(
        body,
        mesh=mesh,
        in_specs=(P("speech", "text"), P(("text", "speech"), None), P("text"), P("speech", "text")),
        out_specs=(P("speech", "text"), P(("text", "speech"), None)),
        check_vma=False,
    )
```

```python
import functools
import math

import jax
import jax.numpy as jnp
from jax import lax
from jax.experimental import pallas as pl
from jax.experimental.pallas import tpu as pltpu
from jax.sharding import PartitionSpec as P

LONG, SHORT = 10**11, 10**9
WORK = {
    "plan_early": LONG,
    "plan_late": 3 * SHORT,
    "plan_part": SHORT,
    "plan_more": SHORT,
    "moments": 3 * SHORT,
    "text_far": 3 * SHORT,
    "text_near": 3 * SHORT,
    "finish": SHORT,
    "frames_first": SHORT,
    "split": SHORT,
    "offsets": SHORT // 10,
    "add": LONG,
}
VMEM_LIMIT = 16 * 1024 * 1024
LANES = 128
IN_VMEM = pl.BlockSpec(memory_space=pltpu.VMEM)
IN_SMEM = pl.BlockSpec(memory_space=pltpu.SMEM)
ANYWHERE = pl.BlockSpec(memory_space=pl.ANY)


def halves(value):
    high = value.astype(jnp.bfloat16)
    low = (value - high.astype(jnp.float32)).astype(jnp.bfloat16)
    return (high, low)


def dot(left, right):
    return lax.dot_general(left, right, (((1,), (0,)), ((), ())), preferred_element_type=jnp.float32)


def dot3(left, right):
    return dot(left[0], right[0]) + dot(left[0], right[1]) + dot(left[1], right[0])


def call(kernel, name, operands, outs, places=0, before=(), scratch=()):
    several = isinstance(outs, list)
    shapes = [jax.ShapeDtypeStruct(shape, kind) for shape, kind in (outs if several else [outs])]
    count = len(operands)

    def body(*refs):
        kernel(*refs[:count], *refs[count + len(before) :])

    return pl.pallas_call(
        body,
        in_specs=[IN_SMEM] * places + [IN_VMEM] * (count - places) + [ANYWHERE] * len(before),
        out_shape=shapes if several else shapes[0],
        scratch_shapes=list(scratch),
        compiler_params=pltpu.CompilerParams(vmem_limit_bytes=VMEM_LIMIT),
        cost_estimate=pl.CostEstimate(flops=WORK.get(name, 0), bytes_accessed=0, transcendentals=0),
        name=name,
    )(*operands, *before)


def copy_kernel(value, out):
    out[...] = value[...]


def add_kernel(*refs):
    *terms, out = refs
    total = terms[0][...]
    for term in terms[1:]:
        total = total + term[...]
    out[...] = total


def group_of(n_text, width):
    return min(n_text, max(2, LANES // width))


def by_distance(value, place, group, lanes):
    count = value.shape[1] // lanes
    step = 1
    while step < count:
        pieces = [value[:, (i ^ step) * lanes : (i ^ step) * lanes + lanes] for i in range(count)]
        odd = (place[0] // (group * step)) % 2 == 1
        value = jnp.where(odd, jnp.concatenate(pieces, axis=1), value)
        step *= 2
    return value


def split_kernel(n_text, group, place, block, high_out, low_out, across_high, across_low):
    value = block[...]
    across_high[...], across_low[...] = halves(value.T)
    lanes = block.shape[1] // n_text * group
    high_out[...], low_out[...] = halves(by_distance(value, place, group, lanes))


def split_block(place, block, n_text):
    rows, feats = block.shape
    group = group_of(n_text, feats // n_text)
    plain, across = ((rows, feats), jnp.bfloat16), ((feats, rows), jnp.bfloat16)
    body = functools.partial(split_kernel, n_text, group)
    return call(body, "split", [place, block], [plain, plain, across, across], places=1)


def assemble(place, group, first, chunks, left):
    width, frames = chunks[0].shape[0] // 2, chunks[0].shape[1]
    for k, chunk in enumerate(chunks, first):
        row = (k - k % group) * width + (place[0] ^ k) % group * width
        here = pl.ds(pl.multiple_of(row, width), width)
        for part in range(2):
            columns = slice(part * frames, (part + 1) * frames)
            left[0][here, columns], left[1][here, columns] = halves(chunk[part * width : (part + 1) * width, :])


def offsets_kernel(place, pot, out):
    count, rows = pot.shape
    for r in range(count):
        row = pot[pl.ds(place[1] ^ r, 1), :]
        out[r * rows : (r + 1) * rows, :] = jnp.broadcast_to(row, (out.shape[1], rows)).T


def plan_rows(scale, first, pot, blocks, left, partials, plan_out, dots_out, sums_out):
    count = len(blocks) // 2
    frames = plan_out.shape[1]
    rows = blocks[0].shape[0]
    for r in range(count):
        here = slice(r * rows, (r + 1) * rows)
        known = left[0].shape[0] // 2 if r < len(partials) else 0
        text = (blocks[r][:, known:], blocks[count + r][:, known:])
        product = dot3(text, (left[0][known:, :], left[1][known:, :]))
        if known:
            product = product + partials[r][...]
        offsets = pot[(first + r) * rows : (first + r + 1) * rows, :]
        lanes = offsets.shape[1]
        plan = jnp.concatenate(
            [jnp.exp(offsets + scale * product[:, i : i + lanes]) for i in range(0, frames, lanes)], axis=1
        )
        grad_dots = product[:, frames:]
        plan_out[here, :] = plan
        dots_out[here, :] = grad_dots
        sums_out[0:1, :] += jnp.sum(plan, axis=0, keepdims=True)
        sums_out[1:2, :] += jnp.sum(plan * grad_dots, axis=0, keepdims=True)


def part_kernel(n_chunks, group, place, *refs):
    chunks, refs = refs[:n_chunks], refs[n_chunks:]
    count = (len(refs) - 2) // 3
    blocks, outs, left = refs[: 2 * count], refs[2 * count : -2], refs[-2:]
    assemble(place, group, 0, chunks, left)
    known = left[0].shape[0]
    for r in range(count):
        text = (blocks[r][:, :known], blocks[count + r][:, :known])
        outs[r][...] = dot3(text, (left[0][...], left[1][...]))


def more_kernel(left_high, left_low, high, low, out):
    known = left_high.shape[0]
    out[...] = dot3((high[:, :known], low[:, :known]), (left_high[...], left_low[...]))


def early_kernel(n_chunks, n_partials, group, scale, place, pot, *refs):
    known, refs = refs[:2], refs[2:]
    chunks, refs = refs[:n_chunks], refs[n_chunks:]
    partials, blocks = refs[:n_partials], refs[n_partials:-5]
    plan_out, dots_out, sums_out, *left = refs[-5:]
    for old, new in zip(known, left):
        new[: old.shape[0], :] = old[...]
    assemble(place, group, n_chunks, chunks, left)
    sums_out[...] = jnp.zeros_like(sums_out)
    plan_rows(scale, 0, pot, blocks, left, partials, plan_out, dots_out, sums_out)


def late_kernel(n_partials, scale, first, pot, sums, left_high, left_low, *refs):
    partials, blocks = refs[:n_partials], refs[n_partials:-3]
    plan_out, dots_out, sums_out = refs[-3:]
    sums_out[...] = sums[...]
    plan_rows(scale, first, pot, blocks, (left_high, left_low), partials, plan_out, dots_out, sums_out)


def across_kernel(n_text, group, place, high, low, high_out, low_out):
    lanes = high.shape[0] // n_text * group
    for value, out in ((high, high_out), (low, low_out)):
        across = value[...].astype(jnp.float32).T
        out[...] = by_distance(across, place, group, lanes).astype(jnp.bfloat16)


def weights(sums, plan, grad_dots, scale):
    mass = sums[0:1, :]
    shared = plan / mass
    weighted = scale * (shared * (grad_dots - sums[1:2, :] / mass))
    return (shared, weighted)


def text_kernel(scale, first, sums, plan, grad_dots, right_high, right_low, *outs):
    rows = len(outs) * outs[0].shape[0]
    here = slice(first, first + rows)
    shared, weighted = weights(sums, plan[here, :], grad_dots[here, :], scale)
    shared, weighted = halves(shared), halves(weighted)
    left = [jnp.concatenate([w, s], axis=1) for w, s in zip(weighted, shared)]
    terms = dot3(left, (right_high[...], right_low[...]))
    for i, out in enumerate(outs):
        out[...] = terms[i * out.shape[0] : (i + 1) * out.shape[0], :]


def moments_kernel(first, rows, estimate, plan, grad_dots, high, low, *refs):
    *total, out = refs
    here = slice(first, first + rows)
    tile = plan[here, :]
    centred = tile * (grad_dots[here, :] - estimate[1:2, :] / estimate[0:1, :])
    term = dot3((high[...], low[...]), halves(jnp.concatenate([tile, centred], axis=1)))
    out[...] = total[0][...] + term if total else term


def finish_kernel(n_text, scale, first, place, estimate, sums, total, plan, grad_dots, high, low, *refs):
    *outs, terms = refs
    frames = sums.shape[1]
    mass = sums[0:1, :]
    drift = sums[1:2, :] / mass - estimate[1:2, :] / estimate[0:1, :]
    here = slice(first, first + high.shape[1])
    _, weighted = weights(sums, plan[here, :], grad_dots[here, :], scale)
    terms[...] = dot3((high[...], low[...]), halves(weighted))
    width = total.shape[0] // n_text
    for k in range(n_text):
        here = pl.ds(pl.multiple_of((place[0] ^ k) * width, width), width)
        block = (scale / mass) * (total[here, frames:] - drift * total[here, :frames]) + terms[here, :]
        for half, step in enumerate((1, 2)):
            columns = slice(half * frames // 2, (half + 1) * frames // 2)
            order = [i for i in range(n_text) if not i & step]
            outs[2 * half + (k & step > 0)][order.index(k & ~step)] = block[:, columns]


def halve_kernel(pairs, *refs):
    operands, outs = refs[: 2 * pairs], refs[2 * pairs :]
    start = 0
    for kept, came in zip(operands[::2], operands[1::2]):
        columns = slice(start, start + kept.shape[2])
        for i in range(kept.shape[0]):
            outs[i % 2][i // 2, :, columns] = kept[i] + came[i]
        start += kept.shape[2]


def halve(*operands):
    count, width = operands[0].shape[:2]
    shape = ((count // 2, width, sum(value.shape[2] for value in operands[::2])), jnp.float32)
    keep, send = call(functools.partial(halve_kernel, len(operands) // 2), "near", operands, [shape, shape])
    return (keep, send)


def shards(n_speech, n_text, speech_feat, text_feat, text_pot, map_grad):
    def swap(value, axis, k):
        count = {"speech": n_speech, "text": n_text}[axis]
        return lax.ppermute(value, axis, [(i, i ^ k) for i in range(count)])

    rows, feats = text_feat.shape
    frames, width = speech_feat.shape
    scale = 1.0 / math.sqrt(feats)
    place = jnp.stack([lax.axis_index("text"), lax.axis_index("speech")]).astype(jnp.int32)
    pot = call(
        offsets_kernel,
        "offsets",
        [place, text_pot.reshape(n_speech, rows)],
        ((n_speech * rows, LANES), jnp.float32),
        places=1,
    )

    blocks = [text_feat] + [None] * (n_speech - 1)
    for r in range(2, n_speech, 2):
        blocks[r] = swap(text_feat, "speech", r)
    blocks[1] = swap(text_feat, "speech", 1)
    packed = jnp.concatenate([speech_feat.T, map_grad.T], axis=0)
    packed = call(copy_kernel, "copy", [packed], (packed.shape, packed.dtype), before=[blocks[1]])
    chunks = [packed] + [None] * (n_text - 1)
    split = [split_block(place, blocks[0], n_text), split_block(place, blocks[1], n_text)]
    known, group = n_text // 2, group_of(n_text, width)
    part_tile = ((rows, 2 * frames), jnp.float32)
    part_shape = ((feats // 2, 2 * frames), jnp.bfloat16)
    for k in range(1, n_text):
        if k & (k - 1) == 0:
            chunks[k] = swap(packed, "text", k)
    for k in range(3, n_text):
        if k & (k - 1):
            step = k & -k
            source = chunks[k ^ step]
            wanted = [chunks[1], chunks[2], pot, *(block[0] for block in split)] if step > 1 else []
            if k == n_text - 1:
                *partials, part_high, part_low = call(
                    functools.partial(part_kernel, known, group),
                    "plan_part",
                    [place, *chunks[:known], *(block[0] for block in split), *(block[1] for block in split)],
                    [part_tile] * len(split) + [part_shape, part_shape],
                    places=1,
                )
                wanted = [*wanted, part_high]
            if wanted:
                source = call(copy_kernel, "copy", [source], (source.shape, source.dtype), before=wanted)
            chunks[k] = swap(source, "text", step)
    for r in range(2, n_speech, 2):
        blocks[r + 1] = swap(blocks[r], "speech", 1)
    split += [split_block(place, block, n_text) for block in blocks[2:]]
    highs, lows, across_highs, across_lows = zip(*split)
    for r in range(2, min(n_speech, 3)):
        partials.append(call(more_kernel, "plan_more", [part_high, part_low, highs[r], lows[r]], part_tile))

    half = n_speech // 2
    tile = ((half * rows, frames), jnp.float32)
    outs = [tile, tile, ((8, frames), jnp.float32)]
    left_shape = ((feats, 2 * frames), jnp.bfloat16)
    plan_early, dots_early, sums, *left = call(
        functools.partial(early_kernel, n_text - known, len(partials[:half]), group, scale),
        "plan_early",
        [place, pot, part_high, part_low, *chunks[known:], *partials[:half], *highs[:half], *lows[:half]],
        [*outs, left_shape, left_shape],
        places=1,
    )
    plan_late, dots_late, sums = call(
        functools.partial(late_kernel, len(partials[half:]), scale, half),
        "plan_late",
        [pot, sums, *left, *partials[half:], *highs[half:], *lows[half:]],
        outs,
    )
    plans, dots = (plan_early, plan_late), (dots_early, dots_late)
    estimate = sums
    total = []
    step = 1
    for r in range(n_speech):
        if r < n_speech - 1:
            total = [
                call(
                    functools.partial(moments_kernel, r % half * rows, rows),
                    "moments",
                    [estimate, plans[r // half], dots[r // half], across_highs[r], across_lows[r], *total],
                    ((feats, 2 * frames), jnp.float32),
                    before=[sums],
                )
            ]
        if step < n_text:
            if step == n_text // 2:
                right = call(
                    functools.partial(across_kernel, n_text, group),
                    "frames_first",
                    [place, *left],
                    [(left_shape[0][::-1], jnp.bfloat16)] * 2,
                    places=1,
                    before=[sums],
                )
            crossing = swap(sums, "text", step)
            sums = call(add_kernel, "hop", [sums, crossing], ((8, frames), jnp.float32), before=total)
            step *= 2
    while step < n_text:
        sums = sums + swap(sums, "text", step)
        step *= 2

    def text_part(r, name, before, pieces=1):
        late, first = divmod(r * rows, half * rows)
        return call(
            functools.partial(text_kernel, scale, first),
            name,
            [sums, plans[late], dots[late], *right],
            [((rows // pieces, feats), jnp.float32)] * pieces,
            before=before,
        )

    shape = ((n_text // 2, width, frames // 2), jnp.float32)

    others = []
    for r in range(2, n_speech, 2):
        (term,) = text_part(r + 1, "text_far", [])
        (part,) = text_part(r, "text_far", [term])
        part = part + swap(term, "speech", 1)
        others.append(swap(part, "speech", r))
    keep_a, send_a, keep_b, send_b = call(
        functools.partial(finish_kernel, n_text, scale, (half - 1) * rows),
        "finish",
        [place, estimate, sums, *total, plans[1], dots[1], across_highs[-1], across_lows[-1]],
        [shape] * 4,
        places=1,
        before=[term],
        scratch=[pltpu.VMEM((feats, frames), jnp.float32)],
    )
    crossed = [swap(piece, "speech", 1) for piece in text_part(1, "text_near", [part], 2)]
    keep_a, send_a = halve(keep_a, swap(send_a, "text", 1))
    keep_b, send_b = halve(keep_b, swap(send_b, "text", 2))
    keep, send = halve(keep_a, swap(send_a, "text", 2), keep_b, swap(send_b, "text", 1))
    step = 4
    while 2 * step < n_text:
        keep, send = halve(keep, swap(send, "text", step))
        step *= 2
    (own,) = text_part(0, "text_near", [part])
    text_grad = call(sum_kernel, "add", [own, *others, *crossed], ((rows, feats), jnp.float32))
    speech_block = call(add_kernel, "join", [keep[0], swap(send[0], "text", step)], ((width, frames), jnp.float32), before=[own])
    return (speech_block.T, text_grad)


def sum_kernel(*refs):
    *terms, out = refs
    rows = out.shape[0]
    total = terms[0][...]
    pieces = [term for term in terms if term.shape[0] < rows]
    for term in terms[1 : len(terms) - len(pieces)]:
        total = total + term[...]
    count = rows // len(pieces)
    for i, piece in enumerate(pieces):
        here = slice(i * count, (i + 1) * count)
        out[here, :] = total[here, :] + piece[...]


def solution(mesh):
    body = functools.partial(shards, mesh.shape["speech"], mesh.shape["text"])
    return jax.shard_map(
        body,
        mesh=mesh,
        in_specs=(P("speech", "text"), P(("text", "speech"), None), P("text"), P("speech", "text")),
        out_specs=(P("speech", "text"), P(("text", "speech"), None)),
        check_vma=False,
    )
```

```python
import functools
import math

import jax
import jax.numpy as jnp
from jax import lax
from jax.experimental import pallas as pl
from jax.experimental.pallas import tpu as pltpu
from jax.sharding import PartitionSpec as P

LONG, SHORT = 10**11, 10**9
WORK = {
    "plan_early": LONG,
    "plan_late": 3 * SHORT,
    "plan_part": SHORT,
    "plan_more": SHORT,
    "moments": 3 * SHORT,
    "frames_first": SHORT,
    "split": SHORT,
    "offsets": SHORT // 10,
    "add": LONG,
}
VMEM_LIMIT = 16 * 1024 * 1024
LANES = 128
IN_VMEM = pl.BlockSpec(memory_space=pltpu.VMEM)
IN_SMEM = pl.BlockSpec(memory_space=pltpu.SMEM)
ANYWHERE = pl.BlockSpec(memory_space=pl.ANY)


def halves(value):
    high = value.astype(jnp.bfloat16)
    low = (value - high.astype(jnp.float32)).astype(jnp.bfloat16)
    return (high, low)


def dot(left, right):
    return lax.dot_general(left, right, (((1,), (0,)), ((), ())), preferred_element_type=jnp.float32)


def dot3(left, right):
    return dot(left[0], right[0]) + dot(left[0], right[1]) + dot(left[1], right[0])


def call(kernel, name, operands, outs, places=0, before=(), scratch=()):
    several = isinstance(outs, list)
    shapes = [jax.ShapeDtypeStruct(shape, kind) for shape, kind in (outs if several else [outs])]
    count = len(operands)

    def body(*refs):
        kernel(*refs[:count], *refs[count + len(before) :])

    return pl.pallas_call(
        body,
        in_specs=[IN_SMEM] * places + [IN_VMEM] * (count - places) + [ANYWHERE] * len(before),
        out_shape=shapes if several else shapes[0],
        scratch_shapes=list(scratch),
        compiler_params=pltpu.CompilerParams(vmem_limit_bytes=VMEM_LIMIT),
        cost_estimate=pl.CostEstimate(flops=WORK.get(name, 0), bytes_accessed=0, transcendentals=0),
        name=name,
    )(*operands, *before)


def copy_kernel(value, out):
    out[...] = value[...]


def add_kernel(*refs):
    *terms, out = refs
    total = terms[0][...]
    for term in terms[1:]:
        total = total + term[...]
    out[...] = total


def group_of(n_text, width):
    return min(n_text, max(2, LANES // width))


def by_distance(value, place, group, lanes):
    count = value.shape[1] // lanes
    step = 1
    while step < count:
        pieces = [value[:, (i ^ step) * lanes : (i ^ step) * lanes + lanes] for i in range(count)]
        odd = (place[0] // (group * step)) % 2 == 1
        value = jnp.where(odd, jnp.concatenate(pieces, axis=1), value)
        step *= 2
    return value


def split_kernel(n_text, group, place, block, high_out, low_out, across_high, across_low):
    value = block[...]
    across_high[...], across_low[...] = halves(value.T)
    lanes = block.shape[1] // n_text * group
    high_out[...], low_out[...] = halves(by_distance(value, place, group, lanes))


def split_block(place, block, n_text):
    rows, feats = block.shape
    group = group_of(n_text, feats // n_text)
    plain, across = ((rows, feats), jnp.bfloat16), ((feats, rows), jnp.bfloat16)
    body = functools.partial(split_kernel, n_text, group)
    return call(body, "split", [place, block], [plain, plain, across, across], places=1)


def assemble(place, group, first, chunks, left):
    width, frames = chunks[0].shape[0] // 2, chunks[0].shape[1]
    for k, chunk in enumerate(chunks, first):
        row = (k - k % group) * width + (place[0] ^ k) % group * width
        here = pl.ds(pl.multiple_of(row, width), width)
        for part in range(2):
            columns = slice(part * frames, (part + 1) * frames)
            left[0][here, columns], left[1][here, columns] = halves(chunk[part * width : (part + 1) * width, :])


def offsets_kernel(place, pot, out):
    count, rows = pot.shape
    for r in range(count):
        row = pot[pl.ds(place[1] ^ r, 1), :]
        out[r * rows : (r + 1) * rows, :] = jnp.broadcast_to(row, (out.shape[1], rows)).T


def plan_rows(scale, first, pot, blocks, left, partials, plan_out, dots_out, sums_out):
    count = len(blocks) // 2
    frames = plan_out.shape[1]
    rows = blocks[0].shape[0]
    for r in range(count):
        here = slice(r * rows, (r + 1) * rows)
        known = left[0].shape[0] // 2 if r < len(partials) else 0
        text = (blocks[r][:, known:], blocks[count + r][:, known:])
        product = dot3(text, (left[0][known:, :], left[1][known:, :]))
        if known:
            product = product + partials[r][...]
        offsets = pot[(first + r) * rows : (first + r + 1) * rows, :]
        lanes = offsets.shape[1]
        plan = jnp.concatenate(
            [jnp.exp(offsets + scale * product[:, i : i + lanes]) for i in range(0, frames, lanes)], axis=1
        )
        grad_dots = product[:, frames:]
        plan_out[here, :] = plan
        dots_out[here, :] = grad_dots
        sums_out[0:1, :] += jnp.sum(plan, axis=0, keepdims=True)
        sums_out[1:2, :] += jnp.sum(plan * grad_dots, axis=0, keepdims=True)


def part_kernel(n_chunks, group, place, *refs):
    chunks, refs = refs[:n_chunks], refs[n_chunks:]
    count = (len(refs) - 2) // 3
    blocks, outs, left = refs[: 2 * count], refs[2 * count : -2], refs[-2:]
    assemble(place, group, 0, chunks, left)
    known = left[0].shape[0]
    for r in range(count):
        text = (blocks[r][:, :known], blocks[count + r][:, :known])
        outs[r][...] = dot3(text, (left[0][...], left[1][...]))


def more_kernel(left_high, left_low, high, low, out):
    known = left_high.shape[0]
    out[...] = dot3((high[:, :known], low[:, :known]), (left_high[...], left_low[...]))


def early_kernel(n_chunks, n_partials, group, scale, place, pot, *refs):
    known, refs = refs[:2], refs[2:]
    chunks, refs = refs[:n_chunks], refs[n_chunks:]
    partials, blocks = refs[:n_partials], refs[n_partials:-5]
    plan_out, dots_out, sums_out, *left = refs[-5:]
    for old, new in zip(known, left):
        new[: old.shape[0], :] = old[...]
    assemble(place, group, n_chunks, chunks, left)
    sums_out[...] = jnp.zeros_like(sums_out)
    plan_rows(scale, 0, pot, blocks, left, partials, plan_out, dots_out, sums_out)


def late_kernel(n_partials, scale, first, pot, sums, left_high, left_low, *refs):
    partials, blocks = refs[:n_partials], refs[n_partials:-3]
    plan_out, dots_out, sums_out = refs[-3:]
    sums_out[...] = sums[...]
    plan_rows(scale, first, pot, blocks, (left_high, left_low), partials, plan_out, dots_out, sums_out)


def across_kernel(n_text, group, place, high, low, high_out, low_out):
    lanes = high.shape[0] // n_text * group
    for value, out in ((high, high_out), (low, low_out)):
        across = value[...].astype(jnp.float32).T
        out[...] = by_distance(across, place, group, lanes).astype(jnp.bfloat16)


def weights(sums, plan, grad_dots, scale):
    mass = sums[0:1, :]
    shared = plan / mass
    weighted = scale * (shared * (grad_dots - sums[1:2, :] / mass))
    return (shared, weighted)


def text_kernel(scale, first, pieces, sums, plan, grad_dots, right_high, right_low, *refs):
    came, outs = refs[:pieces], refs[pieces:]
    rows = len(outs) * outs[0].shape[0]
    here = slice(first, first + rows)
    shared, weighted = weights(sums, plan[here, :], grad_dots[here, :], scale)
    shared, weighted = halves(shared), halves(weighted)
    left = [jnp.concatenate([w, s], axis=1) for w, s in zip(weighted, shared)]
    terms = dot3(left, (right_high[...], right_low[...]))
    if came:
        terms = terms + jnp.concatenate([piece[...] for piece in came], axis=0)
    for i, out in enumerate(outs):
        out[...] = terms[i * out.shape[0] : (i + 1) * out.shape[0], :]


def moments_kernel(first, rows, estimate, plan, grad_dots, high, low, *refs):
    *total, out = refs
    here = slice(first, first + rows)
    tile = plan[here, :]
    centred = tile * (grad_dots[here, :] - estimate[1:2, :] / estimate[0:1, :])
    term = dot3((high[...], low[...]), halves(jnp.concatenate([tile, centred], axis=1)))
    out[...] = total[0][...] + term if total else term


def finish_kernel(n_text, scale, firsts, place, estimate, sums, total, plan, grad_dots, *refs):
    blocks, outs, terms = refs[: 2 * len(firsts)], refs[2 * len(firsts) : -1], refs[-1]
    frames = sums.shape[1]
    mass = sums[0:1, :]
    drift = sums[1:2, :] / mass - estimate[1:2, :] / estimate[0:1, :]
    for i, first in enumerate(firsts):
        high, low = blocks[2 * i : 2 * i + 2]
        here = slice(first, first + high.shape[1])
        _, weighted = weights(sums, plan[here, :], grad_dots[here, :], scale)
        term = dot3((high[...], low[...]), halves(weighted))
        terms[...] = terms[...] + term if i else term
    width = total.shape[0] // n_text
    for k in range(n_text):
        here = pl.ds(pl.multiple_of((place[0] ^ k) * width, width), width)
        block = (scale / mass) * (total[here, frames:] - drift * total[here, :frames]) + terms[here, :]
        for half, step in enumerate((1, 2)):
            columns = slice(half * frames // 2, (half + 1) * frames // 2)
            order = [i for i in range(n_text) if not i & step]
            outs[2 * half + (k & step > 0)][order.index(k & ~step)] = block[:, columns]


def halve_kernel(pairs, *refs):
    operands, outs = refs[: 2 * pairs], refs[2 * pairs :]
    start = 0
    for kept, came in zip(operands[::2], operands[1::2]):
        columns = slice(start, start + kept.shape[2])
        for i in range(kept.shape[0]):
            outs[i % 2][i // 2, :, columns] = kept[i] + came[i]
        start += kept.shape[2]


def halve(*operands):
    count, width = operands[0].shape[:2]
    shape = ((count // 2, width, sum(value.shape[2] for value in operands[::2])), jnp.float32)
    keep, send = call(functools.partial(halve_kernel, len(operands) // 2), "near", operands, [shape, shape])
    return (keep, send)


def shards(n_speech, n_text, speech_feat, text_feat, text_pot, map_grad):
    def swap(value, axis, k):
        count = {"speech": n_speech, "text": n_text}[axis]
        return lax.ppermute(value, axis, [(i, i ^ k) for i in range(count)])

    rows, feats = text_feat.shape
    frames, width = speech_feat.shape
    scale = 1.0 / math.sqrt(feats)
    place = jnp.stack([lax.axis_index("text"), lax.axis_index("speech")]).astype(jnp.int32)
    pot = call(
        offsets_kernel,
        "offsets",
        [place, text_pot.reshape(n_speech, rows)],
        ((n_speech * rows, LANES), jnp.float32),
        places=1,
    )

    blocks = [text_feat] + [None] * (n_speech - 1)
    for r in range(2, n_speech, 2):
        blocks[r] = swap(text_feat, "speech", r)
    blocks[1] = swap(text_feat, "speech", 1)
    packed = jnp.concatenate([speech_feat.T, map_grad.T], axis=0)
    packed = call(copy_kernel, "copy", [packed], (packed.shape, packed.dtype), before=[blocks[1]])
    chunks = [packed] + [None] * (n_text - 1)
    split = [split_block(place, blocks[0], n_text), split_block(place, blocks[1], n_text)]
    known, group = n_text // 2, group_of(n_text, width)
    part_tile = ((rows, 2 * frames), jnp.float32)
    part_shape = ((feats // 2, 2 * frames), jnp.bfloat16)
    for k in range(1, n_text):
        if k & (k - 1) == 0:
            chunks[k] = swap(packed, "text", k)
    for k in range(3, n_text):
        if k & (k - 1):
            step = k & -k
            source = chunks[k ^ step]
            wanted = [chunks[1], chunks[2], pot, *(block[0] for block in split)] if step > 1 else []
            if k == n_text - 1:
                *partials, part_high, part_low = call(
                    functools.partial(part_kernel, known, group),
                    "plan_part",
                    [place, *chunks[:known], *(block[0] for block in split), *(block[1] for block in split)],
                    [part_tile] * len(split) + [part_shape, part_shape],
                    places=1,
                )
                wanted = [*wanted, part_high]
            if wanted:
                source = call(copy_kernel, "copy", [source], (source.shape, source.dtype), before=wanted)
            chunks[k] = swap(source, "text", step)
    for r in range(2, n_speech, 2):
        blocks[r + 1] = swap(blocks[r], "speech", 1)
    split += [split_block(place, block, n_text) for block in blocks[2:]]
    highs, lows, across_highs, across_lows = zip(*split)
    for r in range(2, min(n_speech, 3)):
        partials.append(call(more_kernel, "plan_more", [part_high, part_low, highs[r], lows[r]], part_tile))

    half = n_speech // 2
    tile = ((half * rows, frames), jnp.float32)
    outs = [tile, tile, ((8, frames), jnp.float32)]
    left_shape = ((feats, 2 * frames), jnp.bfloat16)
    plan_early, dots_early, sums, *left = call(
        functools.partial(early_kernel, n_text - known, len(partials[:half]), group, scale),
        "plan_early",
        [place, pot, part_high, part_low, *chunks[known:], *partials[:half], *highs[:half], *lows[:half]],
        [*outs, left_shape, left_shape],
        places=1,
    )
    plan_late, dots_late, sums = call(
        functools.partial(late_kernel, len(partials[half:]), scale, half),
        "plan_late",
        [pot, sums, *left, *partials[half:], *highs[half:], *lows[half:]],
        outs,
    )
    plans, dots = (plan_early, plan_late), (dots_early, dots_late)
    estimate = sums
    total = []
    step = 1
    for r in range(n_speech):
        if r < n_speech - 1:
            total = [
                call(
                    functools.partial(moments_kernel, r % half * rows, rows),
                    "moments",
                    [estimate, plans[r // half], dots[r // half], across_highs[r], across_lows[r], *total],
                    ((feats, 2 * frames), jnp.float32),
                    before=[sums],
                )
            ]
        if step < n_text:
            if step == n_text // 2:
                right = call(
                    functools.partial(across_kernel, n_text, group),
                    "frames_first",
                    [place, *left],
                    [(left_shape[0][::-1], jnp.bfloat16)] * 2,
                    places=1,
                    before=[sums],
                )
            crossing = swap(sums, "text", step)
            sums = call(add_kernel, "hop", [sums, crossing], ((8, frames), jnp.float32), before=total)
            step *= 2
    while step < n_text:
        sums = sums + swap(sums, "text", step)
        step *= 2

    def text_part(r, name, before, pieces=1, came=()):
        late, first = divmod(r * rows, half * rows)
        return call(
            functools.partial(text_kernel, scale, first, len(came)),
            name,
            [sums, plans[late], dots[late], *right, *came],
            [((rows // pieces, feats), jnp.float32)] * pieces,
            before=before,
        )

    shape = ((n_text // 2, width, frames // 2), jnp.float32)

    direct = range(n_speech - 1, n_speech)
    others = []
    for r in range(2, n_speech, 2):
        (term,) = text_part(r + 1, "text_far", [])
        (part,) = text_part(r, "text_far", [term])
        part = part + swap(term, "speech", 1)
        others.append(swap(part, "speech", r))
    keep_a, send_a, keep_b, send_b = call(
        functools.partial(finish_kernel, n_text, scale, [(r - half) * rows for r in direct]),
        "finish",
        [place, estimate, sums, *total, plans[1], dots[1], *(across for r in direct for across in split[r][2:])],
        [shape] * 4,
        places=1,
        before=[term],
        scratch=[pltpu.VMEM((feats, frames), jnp.float32)],
    )
    crossed = [swap(piece, "speech", 1) for piece in text_part(1, "text_near", [keep_a], 2)]
    keep_a, send_a = halve(keep_a, swap(send_a, "text", 1))
    keep_b, send_b = halve(keep_b, swap(send_b, "text", 2))
    keep, send = halve(keep_a, swap(send_a, "text", 2), keep_b, swap(send_b, "text", 1))
    step = 4
    while 2 * step < n_text:
        keep, send = halve(keep, swap(send, "text", step))
        step *= 2
    (own,) = text_part(0, "text_near", [part], came=crossed)
    text_grad, speech_block = call(
        last_kernel,
        "add",
        [keep[0], swap(send[0], "text", step), own, *others],
        [((rows, feats), jnp.float32), ((width, frames), jnp.float32)],
    )
    return (speech_block.T, text_grad)


def last_kernel(kept, came, *refs):
    *terms, text_out, speech_out = refs
    speech_out[...] = kept[...] + came[...]
    add_kernel(*terms, text_out)


def solution(mesh):
    body = functools.partial(shards, mesh.shape["speech"], mesh.shape["text"])
    return jax.shard_map(
        body,
        mesh=mesh,
        in_specs=(P("speech", "text"), P(("text", "speech"), None), P("text"), P("speech", "text")),
        out_specs=(P("speech", "text"), P(("text", "speech"), None)),
        check_vma=False,
    )
```

```python
import functools
import math

import jax
import jax.numpy as jnp
from jax import lax
from jax.experimental import pallas as pl
from jax.experimental.pallas import tpu as pltpu
from jax.sharding import PartitionSpec as P

LONG, SHORT = 10**11, 10**9
WORK = {
    "plan_early": LONG,
    "plan_late": 3 * SHORT,
    "plan_part": SHORT,
    "plan_more": SHORT,
    "moments": 6 * SHORT,
    "frames_first": SHORT,
    "split": SHORT,
    "offsets": SHORT // 10,
    "add": LONG,
}
VMEM_LIMIT = 16 * 1024 * 1024
LANES = 128
IN_VMEM = pl.BlockSpec(memory_space=pltpu.VMEM)
IN_SMEM = pl.BlockSpec(memory_space=pltpu.SMEM)
ANYWHERE = pl.BlockSpec(memory_space=pl.ANY)


def halves(value):
    high = value.astype(jnp.bfloat16)
    low = (value - high.astype(jnp.float32)).astype(jnp.bfloat16)
    return (high, low)


def dot(left, right):
    return lax.dot_general(left, right, (((1,), (0,)), ((), ())), preferred_element_type=jnp.float32)


def dot3(left, right):
    return dot(left[0], right[0]) + dot(left[0], right[1]) + dot(left[1], right[0])


def call(kernel, name, operands, outs, places=0, before=(), scratch=()):
    several = isinstance(outs, list)
    shapes = [jax.ShapeDtypeStruct(shape, kind) for shape, kind in (outs if several else [outs])]
    count = len(operands)

    def body(*refs):
        kernel(*refs[:count], *refs[count + len(before) :])

    return pl.pallas_call(
        body,
        in_specs=[IN_SMEM] * places + [IN_VMEM] * (count - places) + [ANYWHERE] * len(before),
        out_shape=shapes if several else shapes[0],
        scratch_shapes=list(scratch),
        compiler_params=pltpu.CompilerParams(vmem_limit_bytes=VMEM_LIMIT),
        cost_estimate=pl.CostEstimate(flops=WORK.get(name, 0), bytes_accessed=0, transcendentals=0),
        name=name,
    )(*operands, *before)


def copy_kernel(value, out):
    out[...] = value[...]


def add_kernel(*refs):
    *terms, out = refs
    total = terms[0][...]
    for term in terms[1:]:
        total = total + term[...]
    out[...] = total


def group_of(n_text, width):
    return min(n_text, max(2, LANES // width))


def by_distance(value, place, group, lanes):
    count = value.shape[1] // lanes
    step = 1
    while step < count:
        pieces = [value[:, (i ^ step) * lanes : (i ^ step) * lanes + lanes] for i in range(count)]
        odd = (place[0] // (group * step)) % 2 == 1
        value = jnp.where(odd, jnp.concatenate(pieces, axis=1), value)
        step *= 2
    return value


def split_kernel(n_text, group, place, block, high_out, low_out, across_high, across_low):
    value = block[...]
    across_high[...], across_low[...] = halves(value.T)
    lanes = block.shape[1] // n_text * group
    high_out[...], low_out[...] = halves(by_distance(value, place, group, lanes))


def split_block(place, block, n_text):
    rows, feats = block.shape
    group = group_of(n_text, feats // n_text)
    plain, across = ((rows, feats), jnp.bfloat16), ((feats, rows), jnp.bfloat16)
    body = functools.partial(split_kernel, n_text, group)
    return call(body, "split", [place, block], [plain, plain, across, across], places=1)


def assemble(place, group, first, chunks, left):
    width, frames = chunks[0].shape[0] // 2, chunks[0].shape[1]
    for k, chunk in enumerate(chunks, first):
        row = (k - k % group) * width + (place[0] ^ k) % group * width
        here = pl.ds(pl.multiple_of(row, width), width)
        for part in range(2):
            columns = slice(part * frames, (part + 1) * frames)
            left[0][here, columns], left[1][here, columns] = halves(chunk[part * width : (part + 1) * width, :])


def offsets_kernel(place, pot, out):
    count, rows = pot.shape
    for r in range(count):
        row = pot[pl.ds(place[1] ^ r, 1), :]
        out[r * rows : (r + 1) * rows, :] = jnp.broadcast_to(row, (out.shape[1], rows)).T


def row_of(sums, i):
    count = sums.shape[0] // 2
    return jnp.concatenate([sums[i * count + j : i * count + j + 1, :] for j in range(count)], axis=1)


def add_to_row(sums, i, row):
    count, lanes = sums.shape[0] // 2, sums.shape[1]
    for j in range(count):
        sums[i * count + j : i * count + j + 1, :] += row[:, j * lanes : (j + 1) * lanes]


def plan_rows(scale, first, pot, blocks, left, partials, plan_out, dots_out, sums_out):
    count = len(blocks) // 2
    frames = plan_out.shape[1]
    rows = blocks[0].shape[0]
    for r in range(count):
        here = slice(r * rows, (r + 1) * rows)
        known = left[0].shape[0] // 2 if r < len(partials) else 0
        text = (blocks[r][:, known:], blocks[count + r][:, known:])
        product = dot3(text, (left[0][known:, :], left[1][known:, :]))
        if known:
            product = product + partials[r][...]
        offsets = pot[(first + r) * rows : (first + r + 1) * rows, :]
        lanes = offsets.shape[1]
        plan = jnp.concatenate(
            [jnp.exp(offsets + scale * product[:, i : i + lanes]) for i in range(0, frames, lanes)], axis=1
        )
        grad_dots = product[:, frames:]
        plan_out[here, :] = plan
        dots_out[here, :] = grad_dots
        add_to_row(sums_out, 0, jnp.sum(plan, axis=0, keepdims=True))
        add_to_row(sums_out, 1, jnp.sum(plan * grad_dots, axis=0, keepdims=True))


def part_kernel(n_chunks, group, place, *refs):
    chunks, refs = refs[:n_chunks], refs[n_chunks:]
    count = (len(refs) - 2) // 3
    blocks, outs, left = refs[: 2 * count], refs[2 * count : -2], refs[-2:]
    assemble(place, group, 0, chunks, left)
    known = left[0].shape[0]
    for r in range(count):
        text = (blocks[r][:, :known], blocks[count + r][:, :known])
        outs[r][...] = dot3(text, (left[0][...], left[1][...]))


def more_kernel(left_high, left_low, high, low, out):
    known = left_high.shape[0]
    out[...] = dot3((high[:, :known], low[:, :known]), (left_high[...], left_low[...]))


def early_kernel(n_chunks, n_partials, group, scale, place, pot, *refs):
    known, refs = refs[:2], refs[2:]
    chunks, refs = refs[:n_chunks], refs[n_chunks:]
    partials, blocks = refs[:n_partials], refs[n_partials:-5]
    plan_out, dots_out, sums_out, *left = refs[-5:]
    for old, new in zip(known, left):
        new[: old.shape[0], :] = old[...]
    assemble(place, group, n_chunks, chunks, left)
    sums_out[...] = jnp.zeros_like(sums_out)
    plan_rows(scale, 0, pot, blocks, left, partials, plan_out, dots_out, sums_out)


def late_kernel(n_partials, scale, first, pot, sums, left_high, left_low, *refs):
    partials, blocks = refs[:n_partials], refs[n_partials:-3]
    plan_out, dots_out, sums_out = refs[-3:]
    sums_out[...] = sums[...]
    plan_rows(scale, first, pot, blocks, (left_high, left_low), partials, plan_out, dots_out, sums_out)


def across_kernel(n_text, group, place, high, low, high_out, low_out):
    lanes = high.shape[0] // n_text * group
    for value, out in ((high, high_out), (low, low_out)):
        across = value[...].astype(jnp.float32).T
        out[...] = by_distance(across, place, group, lanes).astype(jnp.bfloat16)


def weights(sums, plan, grad_dots, scale):
    mass = row_of(sums, 0)
    shared = plan / mass
    weighted = scale * (shared * (grad_dots - row_of(sums, 1) / mass))
    return (shared, weighted)


def text_kernel(scale, first, pieces, sums, plan, grad_dots, right_high, right_low, *refs):
    came, outs = refs[:pieces], refs[pieces:]
    rows = len(outs) * outs[0].shape[0]
    here = slice(first, first + rows)
    shared, weighted = weights(sums, plan[here, :], grad_dots[here, :], scale)
    shared, weighted = halves(shared), halves(weighted)
    left = [jnp.concatenate([w, s], axis=1) for w, s in zip(weighted, shared)]
    terms = dot3(left, (right_high[...], right_low[...]))
    if came:
        terms = terms + jnp.concatenate([piece[...] for piece in came], axis=0)
    for i, out in enumerate(outs):
        out[...] = terms[i * out.shape[0] : (i + 1) * out.shape[0], :]


def moments_kernel(first, rows, estimate, plan, grad_dots, high, low, *refs):
    *total, out = refs
    here = slice(first, first + rows)
    tile = plan[here, :]
    centred = tile * (grad_dots[here, :] - row_of(estimate, 1) / row_of(estimate, 0))
    term = dot3((high[...], low[...]), halves(jnp.concatenate([tile, centred], axis=1)))
    out[...] = total[0][...] + term if total else term


def finish_kernel(n_text, scale, firsts, place, estimate, sums, total, plan, grad_dots, *refs):
    blocks, outs, terms = refs[: 2 * len(firsts)], refs[2 * len(firsts) : -1], refs[-1]
    frames = total.shape[1] // 2
    mass = row_of(sums, 0)
    drift = row_of(sums, 1) / mass - row_of(estimate, 1) / row_of(estimate, 0)
    for i, first in enumerate(firsts):
        high, low = blocks[2 * i : 2 * i + 2]
        here = slice(first, first + high.shape[1])
        _, weighted = weights(sums, plan[here, :], grad_dots[here, :], scale)
        term = dot3((high[...], low[...]), halves(weighted))
        terms[...] = terms[...] + term if i else term
    width = total.shape[0] // n_text
    for k in range(n_text):
        here = pl.ds(pl.multiple_of((place[0] ^ k) * width, width), width)
        block = (scale / mass) * (total[here, frames:] - drift * total[here, :frames]) + terms[here, :]
        for half, step in enumerate((1, 2)):
            columns = slice(half * frames // 2, (half + 1) * frames // 2)
            order = [i for i in range(n_text) if not i & step]
            outs[2 * half + (k & step > 0)][order.index(k & ~step)] = block[:, columns]


def halve_kernel(pairs, *refs):
    operands, outs = refs[: 2 * pairs], refs[2 * pairs :]
    start = 0
    for kept, came in zip(operands[::2], operands[1::2]):
        columns = slice(start, start + kept.shape[2])
        for i in range(kept.shape[0]):
            outs[i % 2][i // 2, :, columns] = kept[i] + came[i]
        start += kept.shape[2]


def halve(*operands):
    count, width = operands[0].shape[:2]
    shape = ((count // 2, width, sum(value.shape[2] for value in operands[::2])), jnp.float32)
    keep, send = call(functools.partial(halve_kernel, len(operands) // 2), "near", operands, [shape, shape])
    return (keep, send)


def shards(n_speech, n_text, speech_feat, text_feat, text_pot, map_grad):
    def swap(value, axis, k):
        count = {"speech": n_speech, "text": n_text}[axis]
        return lax.ppermute(value, axis, [(i, i ^ k) for i in range(count)])

    rows, feats = text_feat.shape
    frames, width = speech_feat.shape
    scale = 1.0 / math.sqrt(feats)
    place = jnp.stack([lax.axis_index("text"), lax.axis_index("speech")]).astype(jnp.int32)
    pot = call(
        offsets_kernel,
        "offsets",
        [place, text_pot.reshape(n_speech, rows)],
        ((n_speech * rows, LANES), jnp.float32),
        places=1,
    )

    blocks = [text_feat] + [None] * (n_speech - 1)
    for r in range(2, n_speech, 2):
        blocks[r] = swap(text_feat, "speech", r)
    blocks[1] = swap(text_feat, "speech", 1)
    packed = jnp.concatenate([speech_feat.T, map_grad.T], axis=0)
    packed = call(copy_kernel, "copy", [packed], (packed.shape, packed.dtype), before=[blocks[1]])
    chunks = [packed] + [None] * (n_text - 1)
    split = [split_block(place, blocks[0], n_text), split_block(place, blocks[1], n_text)]
    known, group = n_text // 2, group_of(n_text, width)
    part_tile = ((rows, 2 * frames), jnp.float32)
    part_shape = ((feats // 2, 2 * frames), jnp.bfloat16)
    for k in range(1, n_text):
        if k & (k - 1) == 0:
            chunks[k] = swap(packed, "text", k)
    for k in range(3, n_text):
        if k & (k - 1):
            step = k & -k
            source = chunks[k ^ step]
            wanted = [chunks[1], chunks[2], pot, *(block[0] for block in split)] if step > 1 else []
            if k == n_text - 1:
                *partials, part_high, part_low = call(
                    functools.partial(part_kernel, known, group),
                    "plan_part",
                    [place, *chunks[:known], *(block[0] for block in split), *(block[1] for block in split)],
                    [part_tile] * len(split) + [part_shape, part_shape],
                    places=1,
                )
                wanted = [*wanted, part_high]
            if wanted:
                source = call(copy_kernel, "copy", [source], (source.shape, source.dtype), before=wanted)
            chunks[k] = swap(source, "text", step)
    for r in range(2, n_speech, 2):
        blocks[r + 1] = swap(blocks[r], "speech", 1)
    split += [split_block(place, block, n_text) for block in blocks[2:]]
    highs, lows, across_highs, across_lows = zip(*split)
    for r in range(2, min(n_speech, 3)):
        partials.append(call(more_kernel, "plan_more", [part_high, part_low, highs[r], lows[r]], part_tile))

    half = n_speech // 2
    tile = ((half * rows, frames), jnp.float32)
    sums_shape = ((2 * frames // LANES, LANES), jnp.float32)
    outs = [tile, tile, sums_shape]
    left_shape = ((feats, 2 * frames), jnp.bfloat16)
    plan_early, dots_early, sums, *left = call(
        functools.partial(early_kernel, n_text - known, len(partials[:half]), group, scale),
        "plan_early",
        [place, pot, part_high, part_low, *chunks[known:], *partials[:half], *highs[:half], *lows[:half]],
        [*outs, left_shape, left_shape],
        places=1,
    )
    plan_late, dots_late, sums = call(
        functools.partial(late_kernel, len(partials[half:]), scale, half),
        "plan_late",
        [pot, sums, *left, *partials[half:], *highs[half:], *lows[half:]],
        outs,
    )
    plans, dots = (plan_early, plan_late), (dots_early, dots_late)
    estimate = sums
    total = []
    step = 1
    for r in range(n_speech):
        if r < n_speech - 1:
            total = [
                call(
                    functools.partial(moments_kernel, r % half * rows, rows),
                    "moments",
                    [estimate, plans[r // half], dots[r // half], across_highs[r], across_lows[r], *total],
                    ((feats, 2 * frames), jnp.float32),
                    before=[sums],
                )
            ]
        if step < n_text:
            if step == n_text // 2:
                right = call(
                    functools.partial(across_kernel, n_text, group),
                    "frames_first",
                    [place, *left],
                    [(left_shape[0][::-1], jnp.bfloat16)] * 2,
                    places=1,
                    before=[sums],
                )
            crossing = swap(sums, "text", step)
            sums = call(add_kernel, "hop", [sums, crossing], sums_shape, before=total)
            step *= 2
    while step < n_text:
        sums = sums + swap(sums, "text", step)
        step *= 2

    def text_part(r, name, before, pieces=1, came=()):
        late, first = divmod(r * rows, half * rows)
        return call(
            functools.partial(text_kernel, scale, first, len(came)),
            name,
            [sums, plans[late], dots[late], *right, *came],
            [((rows // pieces, feats), jnp.float32)] * pieces,
            before=before,
        )

    shape = ((n_text // 2, width, frames // 2), jnp.float32)

    direct = range(n_speech - 1, n_speech)
    others = []
    for r in range(2, n_speech, 2):
        (term,) = text_part(r + 1, "text_far", [])
        (part,) = text_part(r, "text_far", [term])
        part = part + swap(term, "speech", 1)
        others.append(swap(part, "speech", r))
    keep_a, send_a, keep_b, send_b = call(
        functools.partial(finish_kernel, n_text, scale, [(r - half) * rows for r in direct]),
        "finish",
        [place, estimate, sums, *total, plans[1], dots[1], *(across for r in direct for across in split[r][2:])],
        [shape] * 4,
        places=1,
        before=[term],
        scratch=[pltpu.VMEM((feats, frames), jnp.float32)],
    )
    crossed = [swap(piece, "speech", 1) for piece in text_part(1, "text_near", [keep_a], 2)]
    keep_a, send_a = halve(keep_a, swap(send_a, "text", 1))
    keep_b, send_b = halve(keep_b, swap(send_b, "text", 2))
    keep, send = halve(keep_a, swap(send_a, "text", 2), keep_b, swap(send_b, "text", 1))
    step = 4
    while 2 * step < n_text:
        keep, send = halve(keep, swap(send, "text", step))
        step *= 2
    (own,) = text_part(0, "text_near", [part], came=crossed)
    text_grad, speech_block = call(
        last_kernel,
        "add",
        [keep[0], swap(send[0], "text", step), own, *others],
        [((rows, feats), jnp.float32), ((width, frames), jnp.float32)],
    )
    return (speech_block.T, text_grad)


def last_kernel(kept, came, *refs):
    *terms, text_out, speech_out = refs
    speech_out[...] = kept[...] + came[...]
    add_kernel(*terms, text_out)


def solution(mesh):
    body = functools.partial(shards, mesh.shape["speech"], mesh.shape["text"])
    return jax.shard_map(
        body,
        mesh=mesh,
        in_specs=(P("speech", "text"), P(("text", "speech"), None), P("text"), P("speech", "text")),
        out_specs=(P("speech", "text"), P(("text", "speech"), None)),
        check_vma=False,
    )
```

```python
import functools
import math

import jax
import jax.numpy as jnp
from jax import lax
from jax.experimental import pallas as pl
from jax.experimental.pallas import tpu as pltpu
from jax.sharding import PartitionSpec as P

LONG, SHORT = 10**11, 10**9
WORK = {
    "plan_early": LONG,
    "plan_late": 3 * SHORT,
    "plan_part": SHORT,
    "plan_more": SHORT,
    "moments": 6 * SHORT,
    "frames_first": SHORT,
    "split": SHORT,
    "offsets": SHORT // 10,
    "add": LONG,
}
VMEM_LIMIT = 16 * 1024 * 1024
LANES = 128
IN_VMEM = pl.BlockSpec(memory_space=pltpu.VMEM)
IN_SMEM = pl.BlockSpec(memory_space=pltpu.SMEM)
ANYWHERE = pl.BlockSpec(memory_space=pl.ANY)


def halves(value):
    high = value.astype(jnp.bfloat16)
    low = (value - high.astype(jnp.float32)).astype(jnp.bfloat16)
    return (high, low)


def dot(left, right):
    return lax.dot_general(left, right, (((1,), (0,)), ((), ())), preferred_element_type=jnp.float32)


def dot3(left, right):
    return dot(left[0], right[0]) + dot(left[0], right[1]) + dot(left[1], right[0])


def call(kernel, name, operands, outs, places=0, before=(), scratch=()):
    several = isinstance(outs, list)
    shapes = [jax.ShapeDtypeStruct(shape, kind) for shape, kind in (outs if several else [outs])]
    count = len(operands)

    def body(*refs):
        kernel(*refs[:count], *refs[count + len(before) :])

    return pl.pallas_call(
        body,
        in_specs=[IN_SMEM] * places + [IN_VMEM] * (count - places) + [ANYWHERE] * len(before),
        out_shape=shapes if several else shapes[0],
        scratch_shapes=list(scratch),
        compiler_params=pltpu.CompilerParams(vmem_limit_bytes=VMEM_LIMIT),
        cost_estimate=pl.CostEstimate(flops=WORK.get(name, 0), bytes_accessed=0, transcendentals=0),
        name=name,
    )(*operands, *before)


def copy_kernel(value, out):
    out[...] = value[...]


def add_kernel(*refs):
    *terms, out = refs
    total = terms[0][...]
    for term in terms[1:]:
        total = total + term[...]
    out[...] = total


def group_of(n_text, width):
    return min(n_text, max(2, LANES // width))


def by_distance(value, place, group, lanes):
    count = value.shape[1] // lanes
    step = 1
    while step < count:
        pieces = [value[:, (i ^ step) * lanes : (i ^ step) * lanes + lanes] for i in range(count)]
        odd = (place[0] // (group * step)) % 2 == 1
        value = jnp.where(odd, jnp.concatenate(pieces, axis=1), value)
        step *= 2
    return value


def split_kernel(n_text, group, place, block, high_out, low_out, across_high, across_low):
    value = block[...]
    across_high[...], across_low[...] = halves(value.T)
    lanes = block.shape[1] // n_text * group
    high_out[...], low_out[...] = halves(by_distance(value, place, group, lanes))


def split_block(place, block, n_text):
    rows, feats = block.shape
    group = group_of(n_text, feats // n_text)
    plain, across = ((rows, feats), jnp.bfloat16), ((feats, rows), jnp.bfloat16)
    body = functools.partial(split_kernel, n_text, group)
    return call(body, "split", [place, block], [plain, plain, across, across], places=1)


def assemble(place, group, first, chunks, left):
    width, frames = chunks[0].shape[0] // 2, chunks[0].shape[1]
    for k, chunk in enumerate(chunks, first):
        row = (k - k % group) * width + (place[0] ^ k) % group * width
        here = pl.ds(pl.multiple_of(row, width), width)
        for part in range(2):
            columns = slice(part * frames, (part + 1) * frames)
            left[0][here, columns], left[1][here, columns] = halves(chunk[part * width : (part + 1) * width, :])


def offsets_kernel(place, pot, out):
    count, rows = pot.shape
    for r in range(count):
        row = pot[pl.ds(place[1] ^ r, 1), :]
        out[r * rows : (r + 1) * rows, :] = jnp.broadcast_to(row, (out.shape[1], rows)).T


def row_of(sums, i):
    count = sums.shape[0] // 2
    return jnp.concatenate([sums[i * count + j : i * count + j + 1, :] for j in range(count)], axis=1)


def add_to_row(sums, i, row):
    count, lanes = sums.shape[0] // 2, sums.shape[1]
    for j in range(count):
        sums[i * count + j : i * count + j + 1, :] += row[:, j * lanes : (j + 1) * lanes]


def plan_rows(scale, first, pot, blocks, left, partials, plan_out, dots_out, sums_out):
    count = len(blocks) // 2
    frames = plan_out.shape[1]
    rows = blocks[0].shape[0]
    for r in range(count):
        here = slice(r * rows, (r + 1) * rows)
        known = left[0].shape[0] // 2 if r < len(partials) else 0
        text = (blocks[r][:, known:], blocks[count + r][:, known:])
        product = dot3(text, (left[0][known:, :], left[1][known:, :]))
        if known:
            product = product + partials[r][...]
        offsets = pot[(first + r) * rows : (first + r + 1) * rows, :]
        lanes = offsets.shape[1]
        plan = jnp.concatenate(
            [jnp.exp(offsets + scale * product[:, i : i + lanes]) for i in range(0, frames, lanes)], axis=1
        )
        grad_dots = product[:, frames:]
        plan_out[here, :] = plan
        dots_out[here, :] = grad_dots
        add_to_row(sums_out, 0, jnp.sum(plan, axis=0, keepdims=True))
        add_to_row(sums_out, 1, jnp.sum(plan * grad_dots, axis=0, keepdims=True))


def part_kernel(n_chunks, group, place, *refs):
    chunks, refs = refs[:n_chunks], refs[n_chunks:]
    count = (len(refs) - 2) // 3
    blocks, outs, left = refs[: 2 * count], refs[2 * count : -2], refs[-2:]
    assemble(place, group, 0, chunks, left)
    known = left[0].shape[0]
    for r in range(count):
        text = (blocks[r][:, :known], blocks[count + r][:, :known])
        outs[r][...] = dot3(text, (left[0][...], left[1][...]))


def more_kernel(left_high, left_low, high, low, out):
    known = left_high.shape[0]
    out[...] = dot3((high[:, :known], low[:, :known]), (left_high[...], left_low[...]))


def early_kernel(n_chunks, n_partials, group, scale, place, pot, *refs):
    known, refs = refs[:2], refs[2:]
    chunks, refs = refs[:n_chunks], refs[n_chunks:]
    partials, blocks = refs[:n_partials], refs[n_partials:-5]
    plan_out, dots_out, sums_out, *left = refs[-5:]
    for old, new in zip(known, left):
        new[: old.shape[0], :] = old[...]
    assemble(place, group, n_chunks, chunks, left)
    sums_out[...] = jnp.zeros_like(sums_out)
    plan_rows(scale, 0, pot, blocks, left, partials, plan_out, dots_out, sums_out)


def late_kernel(n_partials, scale, first, pot, sums, left_high, left_low, *refs):
    partials, blocks = refs[:n_partials], refs[n_partials:-3]
    plan_out, dots_out, sums_out = refs[-3:]
    sums_out[...] = sums[...]
    plan_rows(scale, first, pot, blocks, (left_high, left_low), partials, plan_out, dots_out, sums_out)


def across_kernel(n_text, group, place, high, low, high_out, low_out):
    lanes = high.shape[0] // n_text * group
    for value, out in ((high, high_out), (low, low_out)):
        across = value[...].astype(jnp.float32).T
        out[...] = by_distance(across, place, group, lanes).astype(jnp.bfloat16)


def weights(sums, plan, grad_dots, scale):
    mass = row_of(sums, 0)
    shared = plan / mass
    weighted = scale * (shared * (grad_dots - row_of(sums, 1) / mass))
    return (shared, weighted)


def text_kernel(scale, first, pieces, sums, plan, grad_dots, right_high, right_low, *refs):
    came, outs = refs[:pieces], refs[pieces:]
    rows = len(outs) * outs[0].shape[0]
    here = slice(first, first + rows)
    shared, weighted = weights(sums, plan[here, :], grad_dots[here, :], scale)
    shared, weighted = halves(shared), halves(weighted)
    left = [jnp.concatenate([w, s], axis=1) for w, s in zip(weighted, shared)]
    terms = dot3(left, (right_high[...], right_low[...]))
    if came:
        terms = terms + jnp.concatenate([piece[...] for piece in came], axis=0)
    for i, out in enumerate(outs):
        out[...] = terms[i * out.shape[0] : (i + 1) * out.shape[0], :]


def moments_kernel(first, rows, estimate, plan, grad_dots, high, low, *refs):
    *total, out = refs
    here = slice(first, first + rows)
    tile = plan[here, :]
    centred = tile * (grad_dots[here, :] - row_of(estimate, 1) / row_of(estimate, 0))
    term = dot3((high[...], low[...]), halves(jnp.concatenate([tile, centred], axis=1)))
    out[...] = total[0][...] + term if total else term


def finish_kernel(n_text, scale, firsts, place, estimate, sums, total, plan, grad_dots, *refs):
    blocks, outs, terms = refs[: 2 * len(firsts)], refs[2 * len(firsts) : -1], refs[-1]
    frames = total.shape[1] // 2
    mass = row_of(sums, 0)
    drift = row_of(sums, 1) / mass - row_of(estimate, 1) / row_of(estimate, 0)
    rows = blocks[0].shape[1]
    here = slice(firsts[0], firsts[0] + len(firsts) * rows)
    _, weighted = weights(sums, plan[here, :], grad_dots[here, :], scale)
    text = [jnp.concatenate([block[...] for block in part], axis=1) for part in (blocks[::2], blocks[1::2])]
    terms[...] = dot3(text, halves(weighted))
    width = total.shape[0] // n_text
    for k in range(n_text):
        here = pl.ds(pl.multiple_of((place[0] ^ k) * width, width), width)
        block = (scale / mass) * (total[here, frames:] - drift * total[here, :frames]) + terms[here, :]
        for half, step in enumerate((1, 2)):
            columns = slice(half * frames // 2, (half + 1) * frames // 2)
            order = [i for i in range(n_text) if not i & step]
            outs[2 * half + (k & step > 0)][order.index(k & ~step)] = block[:, columns]


def halve_kernel(pairs, *refs):
    operands, outs = refs[: 2 * pairs], refs[2 * pairs :]
    start = 0
    for kept, came in zip(operands[::2], operands[1::2]):
        columns = slice(start, start + kept.shape[2])
        for i in range(kept.shape[0]):
            outs[i % 2][i // 2, :, columns] = kept[i] + came[i]
        start += kept.shape[2]


def halve(*operands):
    count, width = operands[0].shape[:2]
    shape = ((count // 2, width, sum(value.shape[2] for value in operands[::2])), jnp.float32)
    keep, send = call(functools.partial(halve_kernel, len(operands) // 2), "near", operands, [shape, shape])
    return (keep, send)


def shards(n_speech, n_text, speech_feat, text_feat, text_pot, map_grad):
    def swap(value, axis, k):
        count = {"speech": n_speech, "text": n_text}[axis]
        return lax.ppermute(value, axis, [(i, i ^ k) for i in range(count)])

    rows, feats = text_feat.shape
    frames, width = speech_feat.shape
    scale = 1.0 / math.sqrt(feats)
    place = jnp.stack([lax.axis_index("text"), lax.axis_index("speech")]).astype(jnp.int32)
    pot = call(
        offsets_kernel,
        "offsets",
        [place, text_pot.reshape(n_speech, rows)],
        ((n_speech * rows, LANES), jnp.float32),
        places=1,
    )

    blocks = [text_feat] + [None] * (n_speech - 1)
    for r in range(2, n_speech, 2):
        blocks[r] = swap(text_feat, "speech", r)
    blocks[1] = swap(text_feat, "speech", 1)
    packed = jnp.concatenate([speech_feat.T, map_grad.T], axis=0)
    packed = call(copy_kernel, "copy", [packed], (packed.shape, packed.dtype), before=[blocks[1]])
    chunks = [packed] + [None] * (n_text - 1)
    split = [split_block(place, blocks[0], n_text), split_block(place, blocks[1], n_text)]
    known, group = n_text // 2, group_of(n_text, width)
    part_tile = ((rows, 2 * frames), jnp.float32)
    part_shape = ((feats // 2, 2 * frames), jnp.bfloat16)
    for k in range(1, n_text):
        if k & (k - 1) == 0:
            chunks[k] = swap(packed, "text", k)
    for k in range(3, n_text):
        if k & (k - 1):
            step = k & -k
            source = chunks[k ^ step]
            wanted = [chunks[1], chunks[2], pot, *(block[0] for block in split)] if step > 1 else []
            if k == n_text - 1:
                *partials, part_high, part_low = call(
                    functools.partial(part_kernel, known, group),
                    "plan_part",
                    [place, *chunks[:known], *(block[0] for block in split), *(block[1] for block in split)],
                    [part_tile] * len(split) + [part_shape, part_shape],
                    places=1,
                )
                wanted = [*wanted, part_high]
            if wanted:
                source = call(copy_kernel, "copy", [source], (source.shape, source.dtype), before=wanted)
            chunks[k] = swap(source, "text", step)
    for r in range(2, n_speech, 2):
        blocks[r + 1] = swap(blocks[r], "speech", 1)
    split += [split_block(place, block, n_text) for block in blocks[2:]]
    highs, lows, across_highs, across_lows = zip(*split)
    for r in range(2, min(n_speech, 3)):
        partials.append(call(more_kernel, "plan_more", [part_high, part_low, highs[r], lows[r]], part_tile))

    half = n_speech // 2
    tile = ((half * rows, frames), jnp.float32)
    sums_shape = ((2 * frames // LANES, LANES), jnp.float32)
    outs = [tile, tile, sums_shape]
    left_shape = ((feats, 2 * frames), jnp.bfloat16)
    plan_early, dots_early, sums, *left = call(
        functools.partial(early_kernel, n_text - known, len(partials[:half]), group, scale),
        "plan_early",
        [place, pot, part_high, part_low, *chunks[known:], *partials[:half], *highs[:half], *lows[:half]],
        [*outs, left_shape, left_shape],
        places=1,
    )
    plan_late, dots_late, sums = call(
        functools.partial(late_kernel, len(partials[half:]), scale, half),
        "plan_late",
        [pot, sums, *left, *partials[half:], *highs[half:], *lows[half:]],
        outs,
    )
    plans, dots = (plan_early, plan_late), (dots_early, dots_late)
    estimate = sums
    total = []
    step = 1
    for r in range(n_speech):
        if r < n_speech - 2:
            total = [
                call(
                    functools.partial(moments_kernel, r % half * rows, rows),
                    "moments",
                    [estimate, plans[r // half], dots[r // half], across_highs[r], across_lows[r], *total],
                    ((feats, 2 * frames), jnp.float32),
                    before=[sums],
                )
            ]
        if step < n_text:
            if step == n_text // 2:
                right = call(
                    functools.partial(across_kernel, n_text, group),
                    "frames_first",
                    [place, *left],
                    [(left_shape[0][::-1], jnp.bfloat16)] * 2,
                    places=1,
                    before=[sums],
                )
            crossing = swap(sums, "text", step)
            sums = call(add_kernel, "hop", [sums, crossing], sums_shape, before=total)
            step *= 2
    while step < n_text:
        sums = sums + swap(sums, "text", step)
        step *= 2

    def text_part(r, name, before, pieces=1, came=()):
        late, first = divmod(r * rows, half * rows)
        return call(
            functools.partial(text_kernel, scale, first, len(came)),
            name,
            [sums, plans[late], dots[late], *right, *came],
            [((rows // pieces, feats), jnp.float32)] * pieces,
            before=before,
        )

    shape = ((n_text // 2, width, frames // 2), jnp.float32)

    direct = range(n_speech - 2, n_speech)
    others = []
    for r in range(2, n_speech, 2):
        (term,) = text_part(r + 1, "text_far", [])
        (part,) = text_part(r, "text_far", [term])
        part = part + swap(term, "speech", 1)
        others.append(swap(part, "speech", r))
    keep_a, send_a, keep_b, send_b = call(
        functools.partial(finish_kernel, n_text, scale, [(r - half) * rows for r in direct]),
        "finish",
        [place, estimate, sums, *total, plans[1], dots[1], *(across for r in direct for across in split[r][2:])],
        [shape] * 4,
        places=1,
        before=[term],
        scratch=[pltpu.VMEM((feats, frames), jnp.float32)],
    )
    crossed = [swap(piece, "speech", 1) for piece in text_part(1, "text_near", [keep_a], 2)]
    keep_a, send_a = halve(keep_a, swap(send_a, "text", 1))
    keep_b, send_b = halve(keep_b, swap(send_b, "text", 2))
    keep, send = halve(keep_a, swap(send_a, "text", 2), keep_b, swap(send_b, "text", 1))
    step = 4
    while 2 * step < n_text:
        keep, send = halve(keep, swap(send, "text", step))
        step *= 2
    (own,) = text_part(0, "text_near", [part], came=crossed)
    text_grad, speech_block = call(
        last_kernel,
        "add",
        [keep[0], swap(send[0], "text", step), own, *others],
        [((rows, feats), jnp.float32), ((width, frames), jnp.float32)],
    )
    return (speech_block.T, text_grad)


def last_kernel(kept, came, *refs):
    *terms, text_out, speech_out = refs
    speech_out[...] = kept[...] + came[...]
    add_kernel(*terms, text_out)


def solution(mesh):
    body = functools.partial(shards, mesh.shape["speech"], mesh.shape["text"])
    return jax.shard_map(
        body,
        mesh=mesh,
        in_specs=(P("speech", "text"), P(("text", "speech"), None), P("text"), P("speech", "text")),
        out_specs=(P("speech", "text"), P(("text", "speech"), None)),
        check_vma=False,
    )
```
